128 devices in a mesh: layer: 2 (over y_hi), row: 8 (over z, core), col: 8 (over y_lo, x).
Axes of the slice: x: 4, y: 4 (y_hi: 2, y_lo: 2; y = y_hi * 2 + y_lo), z: 4, core: 2. Of those that a mesh axis runs over, the one named last changes fastest.
Arguments:
- rhs: bfloat16 [4, 8, 256, 512], P(None, 'row'), may hold values from -6 to 6
- dinv: bfloat16 [4, 8, 512, 512], P(None, 'row'), may hold values from -3 to 3
- factor: bfloat16 [3, 8, 192, 512, 512], P(None, 'row', ('layer', 'col')), may hold values from -0.02734375 to 0.02734375
- deps: int32 [3, 8, 192], P(None, 'row', ('layer', 'col')), may hold values from 0 to 23, as said below
- counts: int32 [3, 8, 16], P(None, 'row', ('layer', 'col')), may hold values from 0 to 12
- sizes: int32 [4, 8], P(None, 'row'), may hold values from 128 to 512
Outputs:
- forward: bfloat16 [4, 8, 256, 512], P(None, 'row')
- solution: bfloat16 [4, 8, 256, 512], P(None, 'row')
The draws below stay inside these ranges and needn't reach their ends.
Inputs may be any that keep to these rules, and one draw needn't show every extreme that they name: `deps`: a slot of block-row (l, r) at index l - 1 names a block of an earlier level, l2 * 8 + r2 with l2 < l; several slots may name one block.
All inputs are finite; a program needn't handle non-finite values.
Results may differ from the reference program's by a relative error of at most 0.013.
Values may be sent and summed in bfloat16 or wider, within the bound.
A program may use at most 128 MiB of HBM per device.

```python
import math
import jax
import jax.numpy as jnp
from jax import lax

B = 512
NRHS = 256
LEV = 4
SPD = 12
NBR = 8
GROUP = 16
SLOTS = 192


def draw_dinv(key, part):
    key = jax.random.fold_in(key, 11)
    first, second = jax.random.split(key)
    off = jax.random.truncated_normal(first, -4.0, 4.0, (LEV, NBR, B, B), jnp.float32) * (0.5 / math.sqrt(B))
    scales = jnp.exp(jax.random.uniform(second, (LEV, NBR, B), jnp.float32, math.log(0.5), math.log(2.0)))
    identity = jnp.eye(B, dtype=jnp.float32)
    return (off + identity * scales[..., None]).astype(jnp.bfloat16)


def draw_deps(key, part):
    key = jax.random.fold_in(key, 7)
    limit = (jnp.arange(LEV - 1, dtype=jnp.int32) + 1) * NBR
    return jax.random.randint(key, (LEV - 1, NBR, SLOTS), 0, limit[:, None, None]).astype(jnp.int32)


def draw_counts(key, part):
    key = jax.random.fold_in(key, 5)
    first, second, third = jax.random.split(key, 3)
    heavy = jax.random.randint(first, (1, NBR, GROUP), 0, SPD + 1)
    each = jax.random.randint(second, (LEV - 1, NBR, GROUP), 0, SPD + 1)
    values = ((heavy * each + SPD - 1) // SPD).reshape(-1)
    total = (LEV - 1) * NBR * GROUP
    spot = jax.random.randint(third, (), 0, total)
    values = jnp.where(jnp.arange(total, dtype=jnp.int32) == spot, SPD, values)
    return values.reshape(LEV - 1, NBR, GROUP).astype(jnp.int32)


def draw_sizes(key, part):
    key = jax.random.fold_in(key, 9)
    first, second = jax.random.split(key)
    values = jax.random.randint(first, (LEV * NBR,), B // 4, B + 1)
    spot = jax.random.randint(second, (), 0, LEV * NBR)
    values = jnp.where(jnp.arange(LEV * NBR, dtype=jnp.int32) == spot, B, values)
    return values.reshape(LEV, NBR).astype(jnp.int32)


def block_scale(own_key, dims, shards, least, top_value):
    loudness = 1.0
    for axis_at, blocks in shards:
        heights = jax.random.uniform(jax.random.fold_in(jax.random.fold_in(own_key, 6), axis_at), (blocks,), jnp.float32, least / len(shards), top_value / len(shards))
        loudness = loudness * jnp.repeat(jnp.exp(heights), dims[axis_at] // blocks).reshape((-1,) + (1,) * (len(dims) - 1 - axis_at))
    return loudness


def noise(own_key, shape, deviation, reach, pieces=(), kind=jnp.bfloat16):
    array = deviation * jax.random.normal(own_key, shape, jnp.float32)
    if pieces:
        array = array * block_scale(own_key, shape, pieces, -0.22, 0.18)
    return jnp.clip(array, -reach, reach).astype(kind)


def setup_inputs(seed: int = 0) -> dict:
    key_of = jax.random.split(jax.random.key(seed), 7)
    return {
        "rhs": noise(key_of[0], (LEV, NBR, NRHS, B), 1.0, 6.0, ((1, 8),)),
        "dinv": draw_dinv(jax.random.fold_in(key_of[6], 71), 0),
        "factor": noise(key_of[2], (LEV - 1, NBR, SLOTS, B, B), (B * SLOTS // 2) ** -0.5, 0.02734375, ((1, 8), (2, 16))),
        "deps": draw_deps(jax.random.fold_in(key_of[6], 71), 0),
        "counts": draw_counts(jax.random.fold_in(key_of[6], 71), 0),
        "sizes": draw_sizes(jax.random.fold_in(key_of[6], 71), 0),
    }


def reference(rhs, dinv, factor, deps, counts, sizes):
    live = (jnp.arange(B, dtype=jnp.int32)[None, None, :] < sizes[:, :, None]).astype(jnp.float32)
    slot_live = (jnp.arange(SLOTS, dtype=jnp.int32)[None, None, :] % SPD < jnp.repeat(counts, SPD, axis=2)).astype(jnp.float32)
    forward = []
    for level in range(LEV):
        rows = []
        for r in range(NBR):
            if level == 0:
                partial_value = jnp.zeros((NRHS, B), jnp.float32)
            else:
                known = jnp.concatenate(forward, axis=0)
                picked = known[deps[level - 1, r]].astype(jnp.float32) * slot_live[level - 1, r][:, None, None]
                partial_value = jnp.einsum("kni,kji->nj", picked, factor[level - 1, r].astype(jnp.float32))
            resid = (rhs[level, r].astype(jnp.float32) - partial_value).astype(jnp.bfloat16)
            product = lax.dot_general(resid, dinv[level, r], (((1,), (1,)), ((), ())), preferred_element_type=jnp.float32)
            rows.append((product * live[level, r][None, :]).astype(jnp.bfloat16))
        forward.append(jnp.stack(rows))
    carried = jnp.zeros((LEV * NBR, NRHS, B), jnp.float32)
    solution = [None] * LEV
    for level in range(LEV - 1, -1, -1):
        rows = []
        for r in range(NBR):
            resid = (forward[level][r].astype(jnp.float32) - carried[level * NBR + r]).astype(jnp.bfloat16)
            product = jnp.dot(resid, dinv[level, r], preferred_element_type=jnp.float32)
            rows.append((product * live[level, r][None, :]).astype(jnp.bfloat16))
        solved = jnp.stack(rows)
        solution[level] = solved
        if level > 0:
            for r in range(NBR):
                terms = jnp.einsum("nj,kji->kni", solved[r].astype(jnp.float32), factor[level - 1, r].astype(jnp.float32))
                terms = terms * slot_live[level - 1, r][:, None, None]
                carried = carried.at[deps[level - 1, r]].add(terms)
    return jnp.stack(forward), jnp.stack(solution)
```

```python
import jax
import jax.numpy as jnp
from jax import lax
from jax.experimental import pallas as pl
from jax.experimental.pallas import tpu as pltpu
from jax.sharding import PartitionSpec as P

MESH = pl.DeviceIdType.MESH
BF = jnp.bfloat16
F32 = jnp.float32
LEV = 4
SPD = 12
W = 512
H = 256
LINE = [(i, k, n) for n in range(2) for k in range(4) for i in range(4) if i or k or n]
NEAR = (1, 3, 2)


def rem4(v):
    return lax.rem(v, 4)


def kernel(
    rhs_ref, dinv_ref, factor_ref, deps_ref, counts_ref, sizes_ref,
    forward_ref, solution_ref,
    rhs_v, dinv_v, fac,
    ko0, ko1, ko2, kx0, kx1, kx2,
    share, fshare, part, acc, f1r,
    a_own, a_oth, sb, sr, os, r1, s2, rr, sol, fw3,
    prev, last,
    in_sem, fac_sem, out_sem,
    plane_send, f1_recv, ag_recv,
    line_send, s1_recv, rs2_recv,
    axis_send, f5_recv, rs1_recv,
    sib_send, f6_recv, sib_recv,
):
    layer, row, col = lax.axis_index("layer"), lax.axis_index("row"), lax.axis_index("col")
    x = rem4(col)
    y = layer * 2 + lax.div(col, 4)
    z = lax.div(row, 2)
    core = lax.rem(row, 2)
    other = 1 - core
    me = core * 4 + z
    know_own, know_oth = (ko0, ko1, ko2), (kx0, kx1, kx2)

    def device(i, j, k, n):
        xx, yy, zz, cc = rem4(x + i), rem4(y + j), rem4(z + k), lax.rem(core + n, 2)
        return (lax.div(yy, 2), zz * 2 + cc, lax.rem(yy, 2) * 4 + xx)

    def send(src, dst, send_sem, recv_sem, to):
        return pltpu.make_async_remote_copy(
            src_ref=src, dst_ref=dst, send_sem=send_sem, recv_sem=recv_sem,
            device_id=to, device_id_type=MESH,
        )

    loads = []
    for level in range(LEV):
        loads.append(pltpu.make_async_copy(
            rhs_ref.at[level, 0, pl.ds(pl.multiple_of((y * 4 + x) * 16, 16), 16)],
            rhs_v.at[level], in_sem.at[level, 0]))
        loads.append(pltpu.make_async_copy(dinv_ref.at[level, 0], dinv_v.at[level], in_sem.at[level, 1]))
    for copy in loads:
        copy.start()
    fac_loads = [
        pltpu.make_async_copy(factor_ref.at[m, 0, k], fac.at[m, k], fac_sem.at[m, k])
        for m in range(LEV - 1) for k in range(SPD)
    ]
    for copy in fac_loads:
        copy.start()

    barrier = pltpu.get_barrier_semaphore()
    partners = [
        (i, j, k, n) for i in range(4) for j in range(4) for k in range(4) for n in range(2)
        if (i or j or k or n) and (i == 0 or j == 0 or (k == 0 and n == 0))
    ]
    for p in partners:
        pl.semaphore_signal(barrier, inc=1, device_id=device(*p), device_id_type=MESH)

    def live_rows(level):
        return (lax.broadcasted_iota(jnp.int32, (1, W), 1) < sizes_ref[level, 0]).astype(F32)

    def plane(src, dst, recv_sem, own):
        copies = []
        for i in range(4):
            for j in range(4):
                if i or j:
                    copies.append(send(
                        src(rem4(y + j), rem4(x + i)), dst, plane_send.at[i, j],
                        recv_sem.at[i, j], device(i, j, 0, 0)))
        for copy in copies:
            copy.start()
        return copies

    def wait(copies):
        for copy in copies:
            copy.wait()

    def prepare():
        def one(m, carry):
            count = counts_ref[m, 0, 0]
            keys = [jnp.where(k < count, deps_ref[m, 0, k], 255) for k in range(SPD)]
            for k in range(SPD):
                at = jnp.int32(SPD)
                for j in range(k):
                    at = jnp.where(keys[j] == keys[k], j, at)
                prev[m, k] = at

            def target(t, carry):
                unit = lax.rem(t, 8)
                name = lax.div(t, 8) * 8 + rem4(unit) * 2 + lax.div(unit, 4)
                at = jnp.int32(SPD)
                for k in range(SPD):
                    at = jnp.where(keys[k] == name, k, at)
                last[m, t] = at
                return carry

            lax.fori_loop(0, 24, target, 0)
            return carry

        lax.fori_loop(0, LEV - 1, one, 0)
        for m in range(LEV - 1):
            a_own[m, SPD] = jnp.zeros((H, H), F32)
            a_oth[m, SPD] = jnp.zeros((H, H), F32)

    def solve_forward(level, resid):
        product = lax.dot_general(
            resid, dinv_v[level], (((1,), (1,)), ((), ())), preferred_element_type=F32)
        solved = (product * live_rows(level)).astype(BF)
        fshare[level] = solved
        return solved

    def gather_level(level, solved):
        own, oth = know_own[level], know_oth[level]
        share[level, 0] = solved[:, :H]
        share[level, 1] = solved[:, H:]
        own[me, y, x] = share[level, core]
        copies = []
        for i, k, n in LINE:
            half = lax.rem(core + n, 2)
            copies.append(send(
                share.at[level, half], own.at[me, y, x], line_send.at[n, k, i],
                s1_recv.at[level, core, k, i],
                device(i * core, i * (1 - core), k, n)))
        for copy in copies:
            copy.start()
        if level == 0:
            prepare()
        for copy in copies:
            copy.wait_send()
        for i, k, n in LINE:
            half = lax.rem(core + n, 2)
            send(share.at[level, half], own.at[me, y, x], line_send.at[n, k, i],
                 s1_recv.at[level, half, k, i], device(0, 0, 0, 1)).wait_recv()
        evens = lambda at: own.at[pl.ds(0, 4), :, at]
        odds = lambda at: own.at[pl.ds(4, 4), at]
        evens_oth = lambda at: oth.at[pl.ds(0, 4), :, at]
        odds_oth = lambda at: oth.at[pl.ds(4, 4), at]
        axis = []
        for i in NEAR:
            axis.append(send(evens(x), evens(x), axis_send.at[0, i], f5_recv.at[level, 0, i], device(i, 0, 0, 0)))
            axis.append(send(odds(y), odds(y), axis_send.at[1, i], f5_recv.at[level, 1, i], device(0, i, 0, 0)))
        for copy in axis:
            copy.start()
        sibling = []

        def pass_on(src, dst, p, i):
            copy = send(src, dst, sib_send.at[p, i], f6_recv.at[level, p, i], device(0, 0, 0, 1))
            copy.start()
            sibling.append(copy)

        pass_on(evens(x), evens_oth(x), 0, 0)
        pass_on(odds(y), odds_oth(y), 1, 0)
        for at, i in enumerate(NEAR):
            axis[2 * at].wait_recv()
            pass_on(evens(rem4(x + 4 - i)), evens_oth(rem4(x + 4 - i)), 0, i)
            axis[2 * at + 1].wait_recv()
            pass_on(odds(rem4(y + 4 - i)), odds_oth(rem4(y + 4 - i)), 1, i)
        for copy in axis:
            copy.wait_send()
        return sibling

    def accumulate(m, know, half):
        def slot(k, carry):
            dep = deps_ref[m - 1, 0, k]
            source = lax.div(dep, 8)
            r = lax.rem(dep, 8)
            unit = lax.rem(r, 2) * 4 + lax.div(r, 2)
            value = know[0][unit].reshape(H, H)
            for at in range(1, m):
                value = jnp.where(source == at, know[at][unit].reshape(H, H), value)
            value = jnp.where(k < counts_ref[m - 1, 0, 0], value, jnp.zeros_like(value))
            block = fac[m - 1, k, :, pl.ds(pl.multiple_of(half * H, H), H)]
            acc[...] += lax.dot_general(
                value, block, (((1,), (1,)), ((), ())), preferred_element_type=F32)
            return carry

        lax.fori_loop(0, SPD, slot, 0)

    for copy in loads[0:2]:
        copy.wait()
    solved = solve_forward(0, rhs_v[0])
    pl.semaphore_wait(barrier, len(partners))
    out_copies = []
    for level in range(LEV - 1):
        sibling = gather_level(level, solved)
        m = level + 1
        for copy in fac_loads[level * SPD : m * SPD]:
            copy.wait()
        acc[...] = jnp.zeros_like(acc)
        accumulate(m, know_own, core)
        wait(sibling)
        accumulate(m, know_oth, other)
        part[...] = acc[...].astype(BF).reshape(4, 4, 16, W)
        f1r[level, y, x] = part[y, x]
        copies = plane(lambda gy, gx: part.at[gy, gx], f1r.at[level, y, x], f1_recv.at[level], None)
        for half, know in ((core, know_own[level]), (other, know_oth[level])):
            out_copies.append(pltpu.make_async_copy(
                know.at[me],
                forward_ref.at[level, :, :, :, pl.ds(pl.multiple_of(half * H, H), H)],
                out_sem.at[len(out_copies)]))
            out_copies[-1].start()
        for copy in loads[2 * m : 2 * m + 2]:
            copy.wait()
        wait(copies)
        total = jnp.sum(f1r[level].astype(F32).reshape(16, 16, W), axis=0)
        solved = solve_forward(m, (rhs_v[m].astype(F32) - total).astype(BF))

    def solve_backward(level, resid):
        product = jnp.dot(resid, dinv_v[level], preferred_element_type=F32)
        return (product * live_rows(level)).astype(BF)

    def contributions(m, half, out):
        def slot(k, carry):
            block = fac[m - 1, k, :, pl.ds(pl.multiple_of(half * H, H), H)]
            term = jnp.dot(sol[m].reshape(H, W), block, preferred_element_type=F32)
            out[m - 1, k] = term + out[m - 1, prev[m - 1, k]]
            return carry

        lax.fori_loop(0, SPD, slot, 0)

    def gathered(level, unit, out):
        value = out[level, last[level, level * 8 + unit]]
        for m in range(level + 2, LEV):
            value = value + out[m - 1, last[m - 1, level * 8 + unit]]
        return value

    last_level = LEV - 1
    fw3[y, x] = solved
    solved = solve_backward(last_level, solved)
    for level in range(last_level, -1, -1):
        sol[level, y, x] = solved
        copies = plane(lambda gy, gx: sol.at[level, y, x], sol.at[level, y, x], ag_recv.at[level], None)
        wait(copies)
        if level == last_level:
            fw_copies = plane(lambda gy, gx: fw3.at[y, x], fw3.at[y, x], f1_recv.at[last_level], None)
        out_copies.append(pltpu.make_async_copy(
            sol.at[level], solution_ref.at[level], out_sem.at[len(out_copies)]))
        out_copies[-1].start()
        if level == 0:
            break
        low = level - 1
        contributions(level, other, a_oth)
        sibling = []

        def to_sibling(unit, carry):
            sb[unit] = gathered(low, unit, a_oth).astype(BF).reshape(4, 4, 16, H)
            send(sb.at[unit], sr.at[unit], sib_send.at[lax.div(unit, 4), rem4(unit)],
                 sib_recv.at[low, unit], device(0, 0, 0, 1)).start()
            return carry

        lax.fori_loop(0, 8, to_sibling, 0)
        contributions(level, core, a_own)

        def from_sibling(unit, carry):
            send(sb.at[unit], sr.at[unit], sib_send.at[lax.div(unit, 4), rem4(unit)],
                 sib_recv.at[low, unit], device(0, 0, 0, 1)).wait()
            both = gathered(low, unit, a_own) + sr[unit].reshape(H, H).astype(F32)
            os[unit] = both.astype(BF).reshape(4, 4, 16, H)
            return carry

        lax.fori_loop(0, 4, from_sibling, 0)
        axis = []
        for i in NEAR:
            axis.append(send(os.at[pl.ds(0, 4), :, rem4(x + i)], r1.at[0, i - 1],
                             axis_send.at[0, i], rs1_recv.at[low, 0, i], device(i, 0, 0, 0)))
        for copy in axis:
            copy.start()
        lax.fori_loop(4, 8, from_sibling, 0)
        for i in NEAR:
            axis.append(send(os.at[pl.ds(4, 4), rem4(y + i)], r1.at[1, i - 1],
                             axis_send.at[1, i], rs1_recv.at[low, 1, i], device(0, i, 0, 0)))
        for copy in axis[3:]:
            copy.start()
        if level == last_level:
            wait(fw_copies)
            out_copies.append(pltpu.make_async_copy(
                fw3, forward_ref.at[last_level], out_sem.at[len(out_copies)]))
            out_copies[-1].start()
        wait(axis[:3])
        for k in range(4):
            s2[0, k] = (os[k, :, x].astype(F32) + r1[0, 0, k].astype(F32)
                        + r1[0, 1, k].astype(F32) + r1[0, 2, k].astype(F32)).astype(BF)
        wait(axis[3:])
        for k in range(4):
            s2[1, k] = (os[4 + k, y].astype(F32) + r1[1, 0, k].astype(F32)
                        + r1[1, 1, k].astype(F32) + r1[1, 2, k].astype(F32)).astype(BF)
        copies = []
        for i, k, n in LINE:
            to = lax.rem(core + n, 2)
            at = rem4(x * to + y * (1 - to) + i)
            copies.append(send(
                s2.at[to, rem4(z + k), at], rr.at[low, core, k, i], line_send.at[n, k, i],
                rs2_recv.at[low, core, k, i], device(i * to, i * (1 - to), k, n)))
        for copy in copies:
            copy.start()
        rr[low, core, 0, 0] = s2[core, z, rem4(x * core + y * (1 - core))]
        for copy in copies:
            copy.wait_send()
        for i, k, n in LINE:
            half = lax.rem(core + n, 2)
            send(s2.at[0, 0, 0], rr.at[low, half, k, i], line_send.at[n, k, i],
                 rs2_recv.at[low, half, k, i], device(0, 0, 0, 1)).wait_recv()
        sums = [jnp.sum(rr[low, half].astype(F32).reshape(16, 16, H), axis=0) for half in range(2)]
        total = jnp.concatenate(sums, axis=1)
        solved = solve_backward(low, (fshare[low].astype(F32) - total).astype(BF))
    for copy in out_copies:
        copy.wait()


def shards(rhs, dinv, factor, deps, counts, sizes):
    any_spec = pl.BlockSpec(memory_space=pl.ANY)
    smem = pl.BlockSpec(memory_space=pltpu.SMEM)
    dma = pltpu.SemaphoreType.DMA
    block = (8, 4, 4, 16, H)
    forward, solved = pl.pallas_call(
        kernel,
        out_shape=[jax.ShapeDtypeStruct((LEV, 4, 4, 16, W), BF)] * 2,
        in_specs=[any_spec] * 3 + [smem] * 3,
        out_specs=[any_spec] * 2,
        scratch_shapes=[
            pltpu.VMEM((LEV, 16, W), BF),
            pltpu.VMEM((LEV, W, W), BF),
            pltpu.VMEM((LEV - 1, SPD, W, W), BF),
        ] + [pltpu.VMEM(block, BF)] * 6 + [
            pltpu.VMEM((LEV, 2, 16, H), BF),
            pltpu.VMEM((LEV, 16, W), BF),
            pltpu.VMEM((4, 4, 16, W), BF),
            pltpu.VMEM((H, W), F32),
            pltpu.VMEM((LEV - 1, 4, 4, 16, W), BF),
            pltpu.VMEM((LEV - 1, SPD + 1, H, H), F32),
            pltpu.VMEM((LEV - 1, SPD + 1, H, H), F32),
            pltpu.VMEM(block, BF),
            pltpu.VMEM(block, BF),
            pltpu.VMEM(block, BF),
            pltpu.VMEM((2, 3, 4, 4, 16, H), BF),
            pltpu.VMEM((2, 4, 4, 16, H), BF),
            pltpu.VMEM((LEV - 1, 2, 4, 4, 16, H), BF),
            pltpu.VMEM((LEV, 4, 4, 16, W), BF),
            pltpu.VMEM((4, 4, 16, W), BF),
            pltpu.SMEM((LEV - 1, SPD), jnp.int32),
            pltpu.SMEM((LEV - 1, 24), jnp.int32),
            dma((LEV, 2)), dma((LEV - 1, SPD)), dma((12,)),
            dma((4, 4)), dma((LEV, 4, 4)), dma((LEV, 4, 4)),
            dma((2, 4, 4)), dma((LEV - 1, 2, 4, 4)), dma((LEV - 1, 2, 4, 4)),
            dma((2, 4)), dma((LEV - 1, 2, 4)), dma((LEV - 1, 2, 4)),
            dma((2, 4)), dma((LEV - 1, 2, 4)), dma((LEV - 1, 8)),
        ],
        compiler_params=pltpu.CompilerParams(
            collective_id=0, has_side_effects=True, vmem_limit_bytes=60 << 20),
        name="levels",
    )(rhs, dinv, factor, deps, counts, sizes)
    return forward.reshape(LEV, 1, H, W), solved.reshape(LEV, 1, H, W)


def solution(mesh):
    placed = (
        P(None, "row", None, None),
        P(None, "row", None, None),
        P(None, "row", ("layer", "col"), None, None),
        P(None, "row", ("layer", "col")),
        P(None, "row", ("layer", "col")),
        P(None, "row"),
    )
    return jax.shard_map(
        shards,
        mesh=mesh,
        in_specs=placed,
        out_specs=(P(None, "row", None, None), P(None, "row", None, None)),
        check_vma=False,
    )
```

```python
import jax
import jax.numpy as jnp
from jax import lax
from jax.experimental import pallas as pl
from jax.experimental.pallas import tpu as pltpu
from jax.sharding import PartitionSpec as P

MESH = pl.DeviceIdType.MESH
BF = jnp.bfloat16
F32 = jnp.float32
LEV = 4
SPD = 12
W = 512
H = 256
UNROLL = 4


def rem4(v):
    return lax.rem(v, 4)


def near_first(v):
    return v + lax.div(v, 2) * (5 - 2 * v)


def kernel(
    rhs_ref, dinv_ref, factor_ref, deps_ref, counts_ref, sizes_ref,
    forward_ref, solution_ref,
    rhs_v, dinv_v, fac, ko, kx, kl,
    share, fshare, part, acc, f1r,
    a, sb, sr, os, r1, s2, rr, sol, fw3,
    prev, last,
    rhs_sem, dinv_sem, fac_sem, fout_sem, sout_sem,
    plane_send, fw3_send, f1_recv, ag_recv, fw3_recv,
    line_send, s1_recv, rs2_recv,
    axis_send, f5_recv, rs1_recv,
    sib_send, f6_recv, sib_recv,
):
    layer, row, col = lax.axis_index("layer"), lax.axis_index("row"), lax.axis_index("col")
    x = rem4(col)
    y = layer * 2 + lax.div(col, 4)
    z = lax.div(row, 2)
    core = lax.rem(row, 2)
    other = 1 - core
    me = core * 4 + z
    line = x * core + y * other

    def device(i, j, k, n):
        xx, yy, zz, cc = rem4(x + i), rem4(y + j), rem4(z + k), lax.rem(core + n, 2)
        return (lax.div(yy, 2), zz * 2 + cc, lax.rem(yy, 2) * 4 + xx)

    def send(src, dst, send_sem, recv_sem, to):
        return pltpu.make_async_remote_copy(
            src_ref=src, dst_ref=dst, send_sem=send_sem, recv_sem=recv_sem,
            device_id=to, device_id_type=MESH,
        )

    def each(low, high, body):
        def step(at, carry):
            body(at)
            return carry
        lax.fori_loop(low, high, step, 0)

    def rows(gy, gx):
        return pl.ds(pl.multiple_of((gy * 4 + gx) * 16, 16), 16)

    def half_cols(half):
        return pl.ds(pl.multiple_of(half * H, H), H)

    mine = rows(y, x)

    def rhs_load(level):
        return pltpu.make_async_copy(rhs_ref.at[level, 0, mine], rhs_v.at[level], rhs_sem.at[level])

    def dinv_load(level):
        return pltpu.make_async_copy(dinv_ref.at[level, 0], dinv_v.at[level], dinv_sem.at[level])

    def fac_load(m):
        return pltpu.make_async_copy(factor_ref.at[m, 0], fac.at[m], fac_sem.at[m])

    def start_loads(level):
        rhs_load(level).start()
        dinv_load(level).start()

    each(0, LEV, start_loads)
    each(0, LEV - 1, lambda m: fac_load(m).start())

    barrier = pltpu.get_barrier_semaphore()

    def greet(i, j, k, n):
        pl.semaphore_signal(barrier, inc=1, device_id=device(i, j, k, n), device_id_type=MESH)

    each(1, 16, lambda o: greet(rem4(o), lax.div(o, 4), 0, 0))
    each(4, 32, lambda o: greet(0, rem4(o), lax.div(o, 8), lax.rem(lax.div(o, 4), 2)))
    each(3, 24, lambda o: greet(
        1 + lax.rem(o, 3), 0, lax.div(o, 6), lax.rem(lax.div(o, 3), 2)))

    def live_rows(level):
        return (lax.broadcasted_iota(jnp.int32, (1, W), 1) < sizes_ref[0, level]).astype(F32)

    def plane_copy(o, src, dst, send_sem, recv_sem):
        i, j = rem4(o), lax.div(o, 4)
        return send(src(rem4(y + j), rem4(x + i)), dst, send_sem.at[o], recv_sem.at[o], device(i, j, 0, 0))

    def part_copy(level):
        return lambda o: plane_copy(
            o, lambda gy, gx: part.at[rows(gy, gx)], f1r.at[level, mine], plane_send, f1_recv.at[level])

    def sol_copy(level):
        return lambda o: plane_copy(
            o, lambda gy, gx: sol.at[level, mine], sol.at[level, mine], plane_send, ag_recv.at[level])

    def fw3_copy(o):
        return plane_copy(o, lambda gy, gx: fw3.at[mine], fw3.at[mine], fw3_send, fw3_recv)

    def prepare():
        def one(m):
            count = counts_ref[0, 0, m]
            keys = [jnp.where(k < count, deps_ref[m, 0, k], 255) for k in range(SPD)]
            for k in range(SPD):
                at = jnp.int32(SPD)
                for j in range(k):
                    at = jnp.where(keys[j] == keys[k], j, at)
                prev[m, k] = at

            def target(t):
                unit = lax.rem(t, 8)
                name = lax.div(t, 8) * 8 + rem4(unit) * 2 + lax.div(unit, 4)
                at = jnp.int32(SPD)
                for k in range(SPD):
                    at = jnp.where(keys[k] == name, k, at)
                last[m, t] = at

            each(0, 24, target)
            a[0, m, SPD] = jnp.zeros((H, H), F32)
            a[1, m, SPD] = jnp.zeros((H, H), F32)

        each(0, LEV - 1, one)

    def solve_forward(level, resid):
        product = lax.dot_general(
            resid, dinv_v[level], (((1,), (1,)), ((), ())), preferred_element_type=F32)
        solved = (product * live_rows(level)).astype(BF)
        fshare[level] = solved
        share[level, 0] = solved[:, :H]
        share[level, 1] = solved[:, H:]

    def accumulate(m, which, half):
        def slot(k, carry):
            dep = deps_ref[m - 1, 0, k]
            r = lax.rem(dep, 8)
            at = dep - r + lax.rem(r, 2) * 4 + lax.div(r, 2)
            value = kl[which, at]
            value = jnp.where(k < counts_ref[0, 0, m - 1], value, jnp.zeros_like(value))
            block = fac[m - 1, k, :, half_cols(half)]
            acc[...] += lax.dot_general(
                value, block, (((1,), (1,)), ((), ())), preferred_element_type=F32)
            return carry

        lax.fori_loop(0, SPD, slot, 0, unroll=UNROLL)

    def forward_out(level, which):
        half = core + which - 2 * core * which
        return pltpu.make_async_copy(
            kl.at[which, level * 8 + me], forward_ref.at[level, :, half_cols(half)],
            fout_sem.at[level, which])

    def forward_level(level):
        slot = lax.rem(level, 2)
        m = level + 1

        def s1(o):
            k, n, i = near_first(lax.div(o, 8)), lax.rem(lax.div(o, 4), 2), rem4(o)
            half = lax.rem(core + n, 2)
            return send(
                share.at[level, half], ko.at[slot, me, y, x], line_send.at[o],
                s1_recv.at[level, core, k, i], device(i * core, i * other, k, n))

        def s1_arrival(k, n, i):
            half = lax.rem(core + n, 2)
            return send(
                share.at[level, half], ko.at[slot, me, y, x], line_send.at[0],
                s1_recv.at[level, half, k, i], device(0, 0, 0, 1))

        def evens(ref, zc, at):
            return ref.at[slot, zc, :, at]

        def odds(ref, zc, at):
            return ref.at[slot, 4 + zc, at]

        def f5(p, k, i):
            zc = rem4(z + 4 - k)
            if p == 0:
                src, to = evens(ko, zc, x), device(i, 0, 0, 0)
            else:
                src, to = odds(ko, zc, y), device(0, i, 0, 0)
            return send(src, src, axis_send.at[p, k, i], f5_recv.at[level, p, k, i], to)

        def f6(p, k, i):
            zc = rem4(z + 4 - k)
            if p == 0:
                at = rem4(x + 4 - i)
                src, dst = evens(ko, zc, at), evens(kx, zc, at)
            else:
                at = rem4(y + 4 - i)
                src, dst = odds(ko, zc, at), odds(kx, zc, at)
            return send(src, dst, sib_send.at[p, k, i], f6_recv.at[level, p, k, i], device(0, 0, 0, 1))

        ko[slot, me, y, x] = share[level, core]
        each(1, 32, lambda o: s1(o).start())

        @pl.when(level == 0)
        def _():
            prepare()

        def chunk(kk):
            k = near_first(kk)
            first = jnp.where(kk == 0, 1, 0)
            each(first, 8, lambda q: s1_arrival(k, lax.div(q, 4), rem4(q)).wait_recv())

            def go(v):
                i = near_first(v)
                f5(0, k, i).start()
                f5(1, k, i).start()

            each(1, 4, go)
            f6(0, k, 0).start()
            f6(1, k, 0).start()

        each(0, 4, chunk)

        def relay(v):
            k, i = near_first(lax.div(v, 3)), near_first(1 + lax.rem(v, 3))
            for p in (0, 1):
                f5(p, k, i).wait_recv()
                f6(p, k, i).start()

        each(0, 12, relay)

        def keep_own(u):
            kl[0, level * 8 + u] = ko[slot, u].reshape(H, H)

        def keep_other(u):
            kl[1, level * 8 + u] = kx[slot, u].reshape(H, H)

        each(0, 8, keep_own)
        fac_load(level).wait()
        acc[...] = jnp.zeros_like(acc)

        def half_pass(which):
            @pl.when(which == 1)
            def _():
                def arrival(v):
                    for p in (0, 1):
                        f6(p, lax.div(v, 4), rem4(v)).wait_recv()
                each(0, 16, arrival)
                each(0, 8, keep_other)
            accumulate(m, which, lax.rem(core + which, 2))

        each(0, 2, half_pass)
        part[...] = acc[...].astype(BF)
        each(1, 16, lambda o: part_copy(level)(o).start())
        f1r[level, mine] = part[mine]
        for which in (0, 1):
            forward_out(level, which).start()
        each(1, 32, lambda o: s1(o).wait_send())

        def sent(v):
            for p in (0, 1):
                f5(p, lax.div(v, 3), 1 + lax.rem(v, 3)).wait_send()

        def passed(v):
            for p in (0, 1):
                f6(p, lax.div(v, 4), rem4(v)).wait_send()

        each(0, 12, sent)
        each(0, 16, passed)
        rhs_load(m).wait()
        dinv_load(m).wait()
        each(1, 16, lambda o: part_copy(level)(o).wait())
        total = jnp.sum(f1r[level].astype(F32).reshape(16, 16, W), axis=0)
        solve_forward(m, (rhs_v[m].astype(F32) - total).astype(BF))

    rhs_load(0).wait()
    dinv_load(0).wait()
    solve_forward(0, rhs_v[0])
    pl.semaphore_wait(barrier, 64)
    each(0, LEV - 1, forward_level)

    def solve_backward(level, resid):
        product = jnp.dot(resid, dinv_v[level], preferred_element_type=F32)
        sol[level, mine] = (product * live_rows(level)).astype(BF)

    def solution_out(level):
        return pltpu.make_async_copy(sol.at[level], solution_ref.at[level], sout_sem.at[level])

    def gather_plane(level):
        each(1, 16, lambda o: sol_copy(level)(o).start())
        each(1, 16, lambda o: sol_copy(level)(o).wait())
        solution_out(level).start()

    def backward_level(it):
        level = LEV - 1 - it
        low = level - 1
        gather_plane(level)

        @pl.when(it == 0)
        def _():
            each(1, 16, lambda o: fw3_copy(o).start())

        def gathered(unit, which):
            value = a[which, 0, last[0, low * 8 + unit]]
            for m in range(1, LEV - 1):
                value = value + a[which, m, last[m, low * 8 + unit]]
            return value

        def pair(unit):
            return send(sb.at[unit], sr.at[unit], sib_send.at[lax.div(unit, 4), rem4(unit), 0],
                        sib_recv.at[low, unit], device(0, 0, 0, 1))

        def far_first(kk):
            return near_first(3 - kk)

        def to_sibling(q):
            unit = lax.rem(q, 2) * 4 + rem4(z + far_first(lax.div(q, 2)))
            sb[unit] = gathered(unit, 0).astype(BF).reshape(4, 4, 16, H)
            pair(unit).start()

        def contributions(which):
            half = lax.rem(core + 1 + which, 2)

            def slot(k, carry):
                block = fac[low, k, :, half_cols(half)]
                term = jnp.dot(sol[level], block, preferred_element_type=F32)
                a[which, low, k] = term + a[which, low, prev[low, k]]
                return carry

            lax.fori_loop(0, SPD, slot, 0, unroll=UNROLL)

            @pl.when(which == 0)
            def _():
                each(0, 8, to_sibling)

        each(0, 2, contributions)

        def rs1(p, k, i):
            zc = rem4(z + k)
            if p == 0:
                src, to = os.at[zc, :, rem4(x + i)], device(i, 0, 0, 0)
            else:
                src, to = os.at[4 + zc, rem4(y + i)], device(0, i, 0, 0)
            return send(src, r1.at[p, i - 1, zc], axis_send.at[p, k, i], rs1_recv.at[low, p, k, i], to)

        def merge(kk):
            k = far_first(kk)
            zc = rem4(z + k)
            for p in (0, 1):
                unit = p * 4 + zc
                pair(unit).wait()
                both = gathered(unit, 1) + sr[unit].reshape(H, H).astype(F32)
                os[unit] = both.astype(BF).reshape(4, 4, 16, H)
                each(1, 4, lambda v: rs1(p, k, v).start())

        each(0, 4, merge)

        def rs2(o):
            k, n, i = lax.div(o, 8), lax.rem(lax.div(o, 4), 2), rem4(o)
            to = lax.rem(core + n, 2)
            at = rem4(x * to + y * (1 - to) + i)
            return send(
                s2.at[to, rem4(z + k), at], rr.at[low, core, k, i], line_send.at[o],
                rs2_recv.at[low, core, k, i], device(i * to, i * (1 - to), k, n))

        def rs2_arrival(o):
            k, n, i = lax.div(o, 8), lax.rem(lax.div(o, 4), 2), rem4(o)
            half = lax.rem(core + n, 2)
            return send(
                s2.at[0, 0, 0], rr.at[low, half, k, i], line_send.at[0],
                rs2_recv.at[low, half, k, i], device(0, 0, 0, 1))

        def fold(kk):
            k = far_first(kk)
            zc = rem4(z + k)
            for p in (0, 1):
                each(1, 4, lambda v: rs1(p, k, v).wait())
                value = os[zc, :, x] if p == 0 else os[4 + zc, y]
                value = value.astype(F32)
                for i in range(3):
                    value = value + r1[p, i, zc].astype(F32)
                s2[p, zc] = value.astype(BF)
            first = jnp.where(kk == 3, 1, 0)
            each(first, 8, lambda q: rs2(k * 8 + q).start())

        each(0, 4, fold)
        rr[low, core, 0, 0] = s2[core, z, line]
        each(1, 32, lambda o: rs2(o).wait_send())
        each(1, 32, lambda o: rs2_arrival(o).wait_recv())
        sums = [jnp.sum(rr[low, half].astype(F32).reshape(16, 16, H), axis=0) for half in range(2)]
        total = jnp.concatenate(sums, axis=1)
        solve_backward(low, (fshare[low].astype(F32) - total).astype(BF))

    fw3[mine] = fshare[LEV - 1]
    solve_backward(LEV - 1, fshare[LEV - 1])
    each(0, LEV - 1, backward_level)
    gather_plane(0)
    each(1, 16, lambda o: fw3_copy(o).wait())
    fw3_out = pltpu.make_async_copy(fw3, forward_ref.at[LEV - 1], fout_sem.at[LEV - 1, 0])
    fw3_out.start()
    each(0, LEV, lambda level: solution_out(level).wait())
    for which in (0, 1):
        each(0, LEV - 1, lambda level: forward_out(level, which).wait())
    fw3_out.wait()


def shards(rhs, dinv, factor, deps, counts, sizes):
    any_spec = pl.BlockSpec(memory_space=pl.ANY)
    smem = pl.BlockSpec(memory_space=pltpu.SMEM)
    dma = pltpu.SemaphoreType.DMA
    block = (8, 4, 4, 16, H)
    forward, solved = pl.pallas_call(
        kernel,
        out_shape=[jax.ShapeDtypeStruct((LEV, H, W), BF)] * 2,
        in_specs=[any_spec] * 3 + [smem] * 3,
        out_specs=[any_spec] * 2,
        scratch_shapes=[
            pltpu.VMEM((LEV, 16, W), BF),
            pltpu.VMEM((LEV, W, W), BF),
            pltpu.VMEM((LEV - 1, SPD, W, W), BF),
            pltpu.VMEM((2,) + block, BF),
            pltpu.VMEM((2,) + block, BF),
            pltpu.VMEM((2, 24, H, H), BF),
            pltpu.VMEM((LEV, 2, 16, H), BF),
            pltpu.VMEM((LEV, 16, W), BF),
            pltpu.VMEM((H, W), BF),
            pltpu.VMEM((H, W), F32),
            pltpu.VMEM((LEV - 1, H, W), BF),
            pltpu.VMEM((2, LEV - 1, SPD + 1, H, H), F32),
            pltpu.VMEM(block, BF),
            pltpu.VMEM(block, BF),
            pltpu.VMEM(block, BF),
            pltpu.VMEM((2, 3, 4, 4, 16, H), BF),
            pltpu.VMEM((2, 4, 4, 16, H), BF),
            pltpu.VMEM((LEV - 1, 2, 4, 4, 16, H), BF),
            pltpu.VMEM((LEV, H, W), BF),
            pltpu.VMEM((H, W), BF),
            pltpu.SMEM((LEV - 1, SPD), jnp.int32),
            pltpu.SMEM((LEV - 1, 24), jnp.int32),
            dma((LEV,)), dma((LEV,)), dma((LEV - 1,)), dma((LEV, 2)), dma((LEV,)),
            dma((16,)), dma((16,)), dma((LEV - 1, 16)), dma((LEV, 16)), dma((16,)),
            dma((32,)), dma((LEV - 1, 2, 4, 4)), dma((LEV - 1, 2, 4, 4)),
            dma((2, 4, 4)), dma((LEV - 1, 2, 4, 4)), dma((LEV - 1, 2, 4, 4)),
            dma((2, 4, 4)), dma((LEV - 1, 2, 4, 4)), dma((LEV - 1, 8)),
        ],
        compiler_params=pltpu.CompilerParams(
            collective_id=0, has_side_effects=True, vmem_limit_bytes=61 << 20),
        name="levels",
    )(rhs, dinv, factor, deps, counts.transpose(1, 2, 0), sizes.T)
    return forward[:, None], solved[:, None]


def solution(mesh):
    placed = (
        P(None, "row", None, None),
        P(None, "row", None, None),
        P(None, "row", ("layer", "col"), None, None),
        P(None, "row", ("layer", "col")),
        P(None, "row", ("layer", "col")),
        P(None, "row"),
    )
    return jax.shard_map(
        shards,
        mesh=mesh,
        in_specs=placed,
        out_specs=(P(None, "row", None, None), P(None, "row", None, None)),
        check_vma=False,
    )
```

```python
import jax
import jax.numpy as jnp
from jax import lax
from jax.experimental import pallas as pl
from jax.experimental.pallas import tpu as pltpu
from jax.sharding import PartitionSpec as P

MESH = pl.DeviceIdType.MESH
BF = jnp.bfloat16
F32 = jnp.float32
LEV = 4
SPD = 12
W = 512
H = 256
UNROLL = 4


def rem4(v):
    return lax.rem(v, 4)


def near_first(v):
    return v + lax.div(v, 2) * (5 - 2 * v)


def kernel(
    rhs_ref, dinv_ref, factor_ref, deps_ref, counts_ref, sizes_ref,
    forward_ref, solution_ref,
    rhs_v, dinv_v, fac, ko, kx, kl,
    share, fshare, part, acc, f1r,
    a, sb, sr, os, r1, s2, rr, sol, fw3,
    spare, prev, last,
    rhs_sem, dinv_sem, fac_sem, fout_sem, sout_sem,
    plane_send, fw3_send, f1_recv, ag_recv, fw3_recv,
    line_send, s1_recv, rs2_recv,
    axis_send, f5_recv, rs1_recv,
    sib_send, f6_recv, sib_recv,
):
    layer, row, col = lax.axis_index("layer"), lax.axis_index("row"), lax.axis_index("col")
    x = rem4(col)
    y = layer * 2 + lax.div(col, 4)
    z = lax.div(row, 2)
    core = lax.rem(row, 2)
    other = 1 - core
    me = core * 4 + z
    line = x * core + y * other

    def device(i, j, k, n):
        xx, yy, zz, cc = rem4(x + i), rem4(y + j), rem4(z + k), lax.rem(core + n, 2)
        return (lax.div(yy, 2), zz * 2 + cc, lax.rem(yy, 2) * 4 + xx)

    def send(src, dst, send_sem, recv_sem, to):
        return pltpu.make_async_remote_copy(
            src_ref=src, dst_ref=dst, send_sem=send_sem, recv_sem=recv_sem,
            device_id=to, device_id_type=MESH,
        )

    def each(low, high, body):
        def step(at, carry):
            body(at)
            return carry
        lax.fori_loop(low, high, step, 0)

    def start_each(low, high, copy):
        def step(at, carry):
            copy(at).start()
            return carry
        lax.fori_loop(low, high, step, 0, unroll=4 if isinstance(high, int) else 1)

    def wait_bytes(kib, sem):
        some = spare.at[pl.ds(0, kib * 2)]
        pltpu.make_async_copy(some, some, sem).wait()

    def rows(gy, gx):
        return pl.ds(pl.multiple_of((gy * 4 + gx) * 16, 16), 16)

    def half_cols(half):
        return pl.ds(pl.multiple_of(half * H, H), H)

    mine = rows(y, x)

    def rhs_load(level):
        return pltpu.make_async_copy(rhs_ref.at[level, 0, mine], rhs_v.at[level], rhs_sem.at[level])

    def dinv_load(level):
        return pltpu.make_async_copy(dinv_ref.at[level, 0], dinv_v.at[level], dinv_sem.at[level])

    def fac_load(m):
        return pltpu.make_async_copy(factor_ref.at[m, 0], fac.at[m], fac_sem.at[m])

    def start_loads(level):
        rhs_load(level).start()
        dinv_load(level).start()

    each(0, LEV, start_loads)
    each(0, LEV - 1, lambda m: fac_load(m).start())

    barrier = pltpu.get_barrier_semaphore()

    def greet(i, j, k, n):
        pl.semaphore_signal(barrier, inc=1, device_id=device(i, j, k, n), device_id_type=MESH)

    each(1, 16, lambda o: greet(rem4(o), lax.div(o, 4), 0, 0))
    each(4, 32, lambda o: greet(0, rem4(o), lax.div(o, 8), lax.rem(lax.div(o, 4), 2)))
    each(3, 24, lambda o: greet(
        1 + lax.rem(o, 3), 0, lax.div(o, 6), lax.rem(lax.div(o, 3), 2)))

    def live_rows(level):
        return (lax.broadcasted_iota(jnp.int32, (1, W), 1) < sizes_ref[0, level]).astype(F32)

    def plane_copy(o, src, dst, send_sem, recv_sem):
        i, j = near_first(rem4(15 - o)), near_first(3 - lax.div(o, 4))
        return send(src(rem4(y + j), rem4(x + i)), dst, send_sem, recv_sem, device(i, j, 0, 0))

    def part_copy(level):
        return lambda o: plane_copy(
            o, lambda gy, gx: part.at[rows(gy, gx)], f1r.at[level, mine], plane_send.at[0], f1_recv.at[level])

    def sol_copy(level):
        return lambda o: plane_copy(
            o, lambda gy, gx: sol.at[level, mine], sol.at[level, mine], plane_send.at[0], ag_recv.at[level])

    def fw3_copy(o):
        return plane_copy(o, lambda gy, gx: fw3.at[mine], fw3.at[mine], fw3_send.at[0], fw3_recv.at[0])

    def prepare():
        def one(m):
            count = counts_ref[0, 0, m]
            keys = [jnp.where(k < count, deps_ref[m, 0, k], 255) for k in range(SPD)]
            for k in range(SPD):
                at = jnp.int32(SPD)
                for j in range(k):
                    at = jnp.where(keys[j] == keys[k], j, at)
                prev[m, k] = at

            def target(t):
                unit = lax.rem(t, 8)
                name = lax.div(t, 8) * 8 + rem4(unit) * 2 + lax.div(unit, 4)
                at = jnp.int32(SPD)
                for k in range(SPD):
                    at = jnp.where(keys[k] == name, k, at)
                last[m, t] = at

            each(0, 24, target)
            a[0, m, SPD] = jnp.zeros((H, H), F32)
            a[1, m, SPD] = jnp.zeros((H, H), F32)

        each(0, LEV - 1, one)

    def solve_forward(level, resid):
        product = lax.dot_general(
            resid, dinv_v[level], (((1,), (1,)), ((), ())), preferred_element_type=F32)
        solved = (product * live_rows(level)).astype(BF)
        fshare[level] = solved
        share[level, 0] = solved[:, :H]
        share[level, 1] = solved[:, H:]

    def accumulate(m, which, half):
        def slot(k, carry):
            dep = deps_ref[m - 1, 0, k]
            r = lax.rem(dep, 8)
            at = dep - r + lax.rem(r, 2) * 4 + lax.div(r, 2)
            value = kl[which, at]
            value = jnp.where(k < counts_ref[0, 0, m - 1], value, jnp.zeros_like(value))
            block = fac[m - 1, k, :, half_cols(half)]
            acc[...] += lax.dot_general(
                value, block, (((1,), (1,)), ((), ())), preferred_element_type=F32)
            return carry

        lax.fori_loop(0, SPD, slot, 0, unroll=UNROLL)

    def forward_out(level, which):
        half = core + which - 2 * core * which
        return pltpu.make_async_copy(
            kl.at[which, level * 8 + me], forward_ref.at[level, :, half_cols(half)],
            fout_sem.at[level, which])

    def forward_level(level):
        slot = lax.rem(level, 2)
        m = level + 1

        def s1(o):
            k, n, i = near_first(lax.div(o, 8)), lax.rem(lax.div(o, 4), 2), near_first(rem4(o))
            half = lax.rem(core + n, 2)
            return send(
                share.at[level, half], ko.at[slot, me, y, x], line_send.at[0],
                s1_recv.at[level, k], device(i * core, i * other, k, n))

        def evens(ref, zc, at):
            return ref.at[slot, zc, :, at]

        def odds(ref, zc, at):
            return ref.at[slot, 4 + zc, at]

        def f5(p, k, i):
            zc = rem4(z + 4 - k)
            if p == 0:
                src, to = evens(ko, zc, x), device(i, 0, 0, 0)
            else:
                src, to = odds(ko, zc, y), device(0, i, 0, 0)
            return send(src, src, axis_send.at[0], f5_recv.at[level, k], to)

        def f6(p, k, i):
            zc = rem4(z + 4 - k)
            if p == 0:
                at = rem4(x + 4 - i)
                src, dst = evens(ko, zc, at), evens(kx, zc, at)
            else:
                at = rem4(y + 4 - i)
                src, dst = odds(ko, zc, at), odds(kx, zc, at)
            return send(src, dst, sib_send.at[0], f6_recv.at[level], device(0, 0, 0, 1))

        own = pltpu.make_async_copy(share.at[level, core], ko.at[slot, me, y, x], s1_recv.at[level, 0])
        own.start()
        start_each(1, 32, s1)

        @pl.when(level == 0)
        def _():
            prepare()

        def chunk(kk):
            k = near_first(kk)
            wait_bytes(64, s1_recv.at[level, k])

            def go(v):
                i = near_first(v)
                f5(0, k, i).start()
                f5(1, k, i).start()

            each(1, 4, go)
            f6(0, k, 0).start()
            f6(1, k, 0).start()

        each(0, 4, chunk)

        def relay(kk):
            k = near_first(kk)
            wait_bytes(192, f5_recv.at[level, k])

            def go(v):
                i = near_first(v)
                f6(0, k, i).start()
                f6(1, k, i).start()

            each(1, 4, go)

        each(0, 4, relay)

        def keep_own(u):
            kl[0, level * 8 + u] = ko[slot, u].reshape(H, H)

        def keep_other(u):
            kl[1, level * 8 + u] = kx[slot, u].reshape(H, H)

        each(0, 8, keep_own)
        fac_load(level).wait()
        acc[...] = jnp.zeros_like(acc)

        def half_pass(which):
            @pl.when(which == 1)
            def _():
                pltpu.make_async_copy(kx.at[slot], kx.at[slot], f6_recv.at[level]).wait()
                each(0, 8, keep_other)
            accumulate(m, which, lax.rem(core + which, 2))

        each(0, 2, half_pass)
        part[...] = acc[...].astype(BF)
        start_each(0, 15, part_copy(level))
        f1r[level, mine] = part[mine]
        for which in (0, 1):
            forward_out(level, which).start()
        wait_bytes(248, line_send.at[0])
        each(0, 4, lambda v: wait_bytes(192, axis_send.at[0]))
        pltpu.make_async_copy(ko.at[slot], ko.at[slot], sib_send.at[0]).wait()
        rhs_load(m).wait()
        dinv_load(m).wait()
        wait_bytes(240, f1_recv.at[level])
        wait_bytes(240, plane_send.at[0])
        total = jnp.sum(f1r[level].astype(F32).reshape(16, 16, W), axis=0)
        solve_forward(m, (rhs_v[m].astype(F32) - total).astype(BF))

    rhs_load(0).wait()
    dinv_load(0).wait()
    solve_forward(0, rhs_v[0])
    pl.semaphore_wait(barrier, 64)
    each(0, LEV - 1, forward_level)

    def solve_backward(level, resid):
        product = jnp.dot(resid, dinv_v[level], preferred_element_type=F32)
        sol[level, mine] = (product * live_rows(level)).astype(BF)

    def solution_out(level):
        return pltpu.make_async_copy(sol.at[level], solution_ref.at[level], sout_sem.at[level])

    def gather_plane(level):
        start_each(0, 15, sol_copy(level))
        wait_bytes(240, ag_recv.at[level])
        wait_bytes(240, plane_send.at[0])
        solution_out(level).start()

    def backward_level(it):
        level = LEV - 1 - it
        low = level - 1
        gather_plane(level)

        @pl.when(it == 0)
        def _():
            start_each(0, 15, fw3_copy)

        def gathered(unit, which):
            value = a[which, 0, last[0, low * 8 + unit]]
            for m in range(1, LEV - 1):
                value = value + a[which, m, last[m, low * 8 + unit]]
            return value

        def pair(unit):
            return send(sb.at[unit], sr.at[unit], sib_send.at[0],
                        sib_recv.at[low, unit], device(0, 0, 0, 1))

        def far_first(kk):
            return near_first(3 - kk)

        def to_sibling(q):
            unit = lax.rem(q, 2) * 4 + rem4(z + far_first(lax.div(q, 2)))
            sb[unit] = gathered(unit, 0).astype(BF).reshape(4, 4, 16, H)
            pair(unit).start()

        def contributions(which):
            half = lax.rem(core + 1 + which, 2)

            def slot(k, carry):
                block = fac[low, k, :, half_cols(half)]
                term = jnp.dot(sol[level], block, preferred_element_type=F32)
                a[which, low, k] = term + a[which, low, prev[low, k]]
                return carry

            lax.fori_loop(0, SPD, slot, 0, unroll=UNROLL)

            @pl.when(which == 0)
            def _():
                each(0, 8, to_sibling)

        each(0, 2, contributions)

        def rs1(p, k, i):
            zc = rem4(z + k)
            if p == 0:
                src, to = os.at[zc, :, rem4(x + i)], device(i, 0, 0, 0)
            else:
                src, to = os.at[4 + zc, rem4(y + i)], device(0, i, 0, 0)
            return send(src, r1.at[p, i - 1, zc], axis_send.at[0], rs1_recv.at[low, p, k], to)

        def merge(kk):
            k = far_first(kk)
            zc = rem4(z + k)
            for p in (0, 1):
                unit = p * 4 + zc
                pair(unit).wait_recv()
                both = gathered(unit, 1) + sr[unit].reshape(H, H).astype(F32)
                os[unit] = both.astype(BF).reshape(4, 4, 16, H)
                start_each(1, 4, lambda v: rs1(p, k, v))

        each(0, 4, merge)

        def rs2(o):
            k, n, i = lax.div(o, 8), lax.rem(lax.div(o, 4), 2), near_first(rem4(o))
            to = lax.rem(core + n, 2)
            at = rem4(x * to + y * (1 - to) + i)
            return send(
                s2.at[to, rem4(z + k), at], rr.at[low, core, k, i], line_send.at[0],
                rs2_recv.at[low], device(i * to, i * (1 - to), k, n))

        def fold(kk):
            k = far_first(kk)
            zc = rem4(z + k)
            for p in (0, 1):
                wait_bytes(96, rs1_recv.at[low, p, k])
                value = os[zc, :, x] if p == 0 else os[4 + zc, y]
                value = value.astype(F32)
                for i in range(3):
                    value = value + r1[p, i, zc].astype(F32)
                s2[p, zc] = value.astype(BF)
            first = jnp.where(kk == 3, 1, 0)
            each(first, 8, lambda q: rs2(k * 8 + q).start())

        each(0, 4, fold)
        rr[low, core, 0, 0] = s2[core, z, line]
        pltpu.make_async_copy(sb, sb, sib_send.at[0]).wait()
        each(0, 4, lambda v: wait_bytes(192, axis_send.at[0]))
        wait_bytes(248, rs2_recv.at[low])
        wait_bytes(248, line_send.at[0])
        sums = [jnp.sum(rr[low, half].astype(F32).reshape(16, 16, H), axis=0) for half in range(2)]
        total = jnp.concatenate(sums, axis=1)
        solve_backward(low, (fshare[low].astype(F32) - total).astype(BF))

    fw3[mine] = fshare[LEV - 1]
    solve_backward(LEV - 1, fshare[LEV - 1])
    each(0, LEV - 1, backward_level)
    gather_plane(0)
    wait_bytes(240, fw3_recv.at[0])
    wait_bytes(240, fw3_send.at[0])
    fw3_out = pltpu.make_async_copy(fw3, forward_ref.at[LEV - 1], fout_sem.at[LEV - 1, 0])
    fw3_out.start()
    each(0, LEV, lambda level: solution_out(level).wait())
    for which in (0, 1):
        each(0, LEV - 1, lambda level: forward_out(level, which).wait())
    fw3_out.wait()


def shards(rhs, dinv, factor, deps, counts, sizes):
    any_spec = pl.BlockSpec(memory_space=pl.ANY)
    smem = pl.BlockSpec(memory_space=pltpu.SMEM)
    dma = pltpu.SemaphoreType.DMA
    block = (8, 4, 4, 16, H)
    forward, solved = pl.pallas_call(
        kernel,
        out_shape=[jax.ShapeDtypeStruct((LEV, H, W), BF)] * 2,
        in_specs=[any_spec] * 3 + [smem] * 3,
        out_specs=[any_spec] * 2,
        scratch_shapes=[
            pltpu.VMEM((LEV, 16, W), BF),
            pltpu.VMEM((LEV, W, W), BF),
            pltpu.VMEM((LEV - 1, SPD, W, W), BF),
            pltpu.VMEM((2,) + block, BF),
            pltpu.VMEM((2,) + block, BF),
            pltpu.VMEM((2, 24, H, H), BF),
            pltpu.VMEM((LEV, 2, 16, H), BF),
            pltpu.VMEM((LEV, 16, W), BF),
            pltpu.VMEM((H, W), BF),
            pltpu.VMEM((H, W), F32),
            pltpu.VMEM((LEV - 1, H, W), BF),
            pltpu.VMEM((2, LEV - 1, SPD + 1, H, H), F32),
            pltpu.VMEM(block, BF),
            pltpu.VMEM(block, BF),
            pltpu.VMEM(block, BF),
            pltpu.VMEM((2, 3, 4, 4, 16, H), BF),
            pltpu.VMEM((2, 4, 4, 16, H), BF),
            pltpu.VMEM((LEV - 1, 2, 4, 4, 16, H), BF),
            pltpu.VMEM((LEV, H, W), BF),
            pltpu.VMEM((H, W), BF),
            pltpu.VMEM((W, 128), F32),
            pltpu.SMEM((LEV - 1, SPD), jnp.int32),
            pltpu.SMEM((LEV - 1, 24), jnp.int32),
            dma((LEV,)), dma((LEV,)), dma((LEV - 1,)), dma((LEV, 2)), dma((LEV,)),
            dma((1,)), dma((1,)), dma((LEV - 1,)), dma((LEV,)), dma((1,)),
            dma((1,)), dma((LEV - 1, 4)), dma((LEV - 1,)),
            dma((1,)), dma((LEV - 1, 4)), dma((LEV - 1, 2, 4)),
            dma((1,)), dma((LEV - 1,)), dma((LEV - 1, 8)),
        ],
        compiler_params=pltpu.CompilerParams(
            collective_id=0, has_side_effects=True, vmem_limit_bytes=61 << 20),
        name="levels",
    )(rhs, dinv, factor, deps, counts.transpose(1, 2, 0), sizes.T)
    return forward[:, None], solved[:, None]


def solution(mesh):
    placed = (
        P(None, "row", None, None),
        P(None, "row", None, None),
        P(None, "row", ("layer", "col"), None, None),
        P(None, "row", ("layer", "col")),
        P(None, "row", ("layer", "col")),
        P(None, "row"),
    )
    return jax.shard_map(
        shards,
        mesh=mesh,
        in_specs=placed,
        out_specs=(P(None, "row", None, None), P(None, "row", None, None)),
        check_vma=False,
    )
```

```python
import jax
import jax.numpy as jnp
from jax import lax
from jax.experimental import pallas as pl
from jax.experimental.pallas import tpu as pltpu
from jax.sharding import PartitionSpec as P

MESH = pl.DeviceIdType.MESH
BF = jnp.bfloat16
F32 = jnp.float32
LEV = 4
SPD = 12
W = 512
H = 256
Q = 128


def rem4(v):
    return lax.rem(v, 4)


def near_first(v):
    return v + lax.div(v, 2) * (5 - 2 * v)


def fold(v):
    n, c = v.shape
    t = v.reshape(n // 8, 8, c)
    return jnp.concatenate([t[:, :, : c // 2], t[:, :, c // 2 :]], axis=1)


def unfold(v):
    n, _, c = v.shape
    return jnp.concatenate([v[:, :8], v[:, 8:]], axis=2).reshape(n * 8, 2 * c)


def kernel(
    rhs_ref, dinv_ref, factor_ref, deps_ref, counts_ref, sizes_ref,
    forward_ref, solution_ref,
    rhs_v, rhs_f, dinv_v, fac, ko, kx, kl,
    share, fshare, part, acc, f1r,
    a, sb, sr, os, r1, s2, rr, solg, sfull, fw3, outs,
    spare, prev, last,
    rhs_sem, dinv_sem, fac_sem, out_sem,
    plane_send, fw3_send, f1_recv, ag_recv, fw3_recv,
    line_send, s1_recv, rs2_recv,
    axis_send, f5_recv, rs1_recv,
    sib_send, f6_recv, sib_recv,
):
    layer, row, col = lax.axis_index("layer"), lax.axis_index("row"), lax.axis_index("col")
    x = rem4(col)
    y = layer * 2 + lax.div(col, 4)
    z = lax.div(row, 2)
    core = lax.rem(row, 2)
    other = 1 - core
    me = core * 4 + z
    line = x * core + y * other

    def device(i, j, k, n):
        xx, yy, zz, cc = rem4(x + i), rem4(y + j), rem4(z + k), lax.rem(core + n, 2)
        return (lax.div(yy, 2), zz * 2 + cc, lax.rem(yy, 2) * 4 + xx)

    def send(src, dst, send_sem, recv_sem, to):
        return pltpu.make_async_remote_copy(
            src_ref=src, dst_ref=dst, send_sem=send_sem, recv_sem=recv_sem,
            device_id=to, device_id_type=MESH,
        )

    def each(low, high, body):
        def step(at, carry):
            body(at)
            return carry
        lax.fori_loop(low, high, step, 0)

    def start_each(low, high, copy):
        def step(at, carry):
            copy(at).start()
            return carry
        lax.fori_loop(low, high, step, 0, unroll=4 if isinstance(low, int) else None)

    def wait_bytes(kib, sem):
        some = spare.at[pl.ds(0, kib * 2)]
        pltpu.make_async_copy(some, some, sem).wait()

    def half_cols(half):
        return pl.ds(pl.multiple_of(half * H, H), H)

    barrier = pltpu.get_barrier_semaphore()

    def greet(i, j, k, n):
        pl.semaphore_signal(barrier, inc=1, device_id=device(i, j, k, n), device_id_type=MESH)

    def rhs_load(level):
        mine = pl.ds(pl.multiple_of((y * 4 + x) * 16, 16), 16)
        return pltpu.make_async_copy(rhs_ref.at[level, 0, mine], rhs_v.at[level], rhs_sem.at[level])

    def dinv_load(level):
        return pltpu.make_async_copy(dinv_ref.at[level, 0], dinv_v.at[level], dinv_sem.at[level])

    def fac_load(m):
        return pltpu.make_async_copy(factor_ref.at[m, 0], fac.at[m], fac_sem.at[m])

    def start_loads(level):
        rhs_load(level).start()
        dinv_load(level).start()

    start_loads(0)
    each(1, 16, lambda o: greet(rem4(o), lax.div(o, 4), 0, 0))
    each(4, 32, lambda o: greet(0, rem4(o), lax.div(o, 8), lax.rem(lax.div(o, 4), 2)))
    each(3, 24, lambda o: greet(
        1 + lax.rem(o, 3), 0, lax.div(o, 6), lax.rem(lax.div(o, 3), 2)))
    each(1, LEV, start_loads)
    each(0, LEV - 1, lambda m: fac_load(m).start())

    def live_rows(level):
        return (lax.broadcasted_iota(jnp.int32, (1, W), 1) < sizes_ref[0, level]).astype(F32)

    def plane_copy(o, src, dst, send_sem, recv_sem):
        i, j = near_first(rem4(15 - o)), near_first(3 - lax.div(o, 4))
        return send(src(rem4(y + j), rem4(x + i)), dst, send_sem, recv_sem, device(i, j, 0, 0))

    def part_copy(level, h):
        return lambda o: plane_copy(
            o, lambda gy, gx: part.at[h, gy, gx], f1r.at[level, h, y, x],
            plane_send.at[h], f1_recv.at[level, h])

    def sol_copy(level, h):
        return lambda o: plane_copy(
            o, lambda gy, gx: solg.at[level, h, y, x], solg.at[level, h, y, x],
            plane_send.at[h], ag_recv.at[level, h])

    def fw3_copy(h):
        return lambda o: plane_copy(
            o, lambda gy, gx: fw3.at[h, y, x], fw3.at[h, y, x], fw3_send.at[h], fw3_recv.at[h])

    def prepare(m):
        count = counts_ref[0, 0, m]
        keys = [jnp.where(k < count, deps_ref[m, 0, k], 255) for k in range(SPD)]
        for k in range(SPD):
            at = jnp.int32(SPD)
            for j in range(k):
                at = jnp.where(keys[j] == keys[k], j, at)
            prev[m, k] = at

        def target(t):
            unit = lax.rem(t, 8)
            name = lax.div(t, 8) * 8 + rem4(unit) * 2 + lax.div(unit, 4)
            at = jnp.int32(SPD)
            for k in range(SPD):
                at = jnp.where(keys[k] == name, k, at)
            last[m, t] = at

        each(0, 24, target)
        for h in (0, 1):
            for which in (0, 1):
                a[h, which, m, SPD] = jnp.zeros((Q, H), F32)

    def solve_forward(level, h, resid):
        product = lax.dot_general(
            resid, dinv_v[level], (((1,), (1,)), ((), ())), preferred_element_type=F32)
        solved = (product * live_rows(level)).astype(BF).astype(F32)
        fshare[level, h] = solved
        share[level, h, 0] = fold(solved[:, :H])[0].astype(BF)
        share[level, h, 1] = fold(solved[:, H:])[0].astype(BF)

    def solve_backward(level, h, resid):
        product = jnp.dot(resid, dinv_v[level], preferred_element_type=F32)
        solg[level, h, y, x] = fold(product * live_rows(level))[0].astype(BF)
        start_each(0, 15, sol_copy(level, h))

    def gather_start(level, h):
        def s1(o):
            k, n, i = near_first(lax.div(o, 8)), lax.rem(lax.div(o, 4), 2), near_first(rem4(o))
            half = lax.rem(core + n, 2)
            return send(
                share.at[level, h, half], ko.at[lax.rem(level, 2), h, me, y, x], line_send.at[h],
                s1_recv.at[level, h, k], device(i * core, i * other, k, n))

        pltpu.make_async_copy(
            share.at[level, h, core], ko.at[lax.rem(level, 2), h, me, y, x],
            s1_recv.at[level, h, 0]).start()
        start_each(1, 32, s1)

    def result_out(at, ref, level):
        return pltpu.make_async_copy(outs.at[at, level], ref.at[level], out_sem.at[at, level])

    def rows_of_both(parts):
        both = [v.reshape(16, 8, v.shape[-1]) for v in parts]
        return jnp.concatenate(both, axis=1).astype(BF).reshape(H, both[0].shape[-1])

    def forward_level(level):
        slot = lax.rem(level, 2)
        m = level + 1

        def evens(ref, h, zc, at):
            return ref.at[slot, h, zc, :, at]

        def odds(ref, h, zc, at):
            return ref.at[slot, h, 4 + zc, at]

        def f5(h, p, k, i):
            zc = rem4(z + 4 - k)
            if p == 0:
                src, to = evens(ko, h, zc, x), device(i, 0, 0, 0)
            else:
                src, to = odds(ko, h, zc, y), device(0, i, 0, 0)
            return send(src, src, axis_send.at[h], f5_recv.at[level, h, k], to)

        def f6(h, p, k, i):
            zc = rem4(z + 4 - k)
            if p == 0:
                at = rem4(x + 4 - i)
                src, dst = evens(ko, h, zc, at), evens(kx, h, zc, at)
            else:
                at = rem4(y + 4 - i)
                src, dst = odds(ko, h, zc, at), odds(kx, h, zc, at)
            return send(src, dst, sib_send.at[h], f6_recv.at[level, h], device(0, 0, 0, 1))

        def spread(h):
            def chunk(kk):
                k = near_first(kk)
                wait_bytes(32, s1_recv.at[level, h, k])

                def go(v):
                    i = near_first(v)
                    f5(h, 0, k, i).start()
                    f5(h, 1, k, i).start()

                each(1, 4, go)
                f6(h, 0, k, 0).start()
                f6(h, 1, k, 0).start()

            each(0, 4, chunk)

        each(0, 2, spread)

        def finish(h):
            def relay(kk):
                k = near_first(kk)
                wait_bytes(96, f5_recv.at[level, h, k])

                def go(v):
                    i = near_first(v)
                    f6(h, 0, k, i).start()
                    f6(h, 1, k, i).start()

                each(1, 4, go)

            each(0, 4, relay)

            @pl.when(h == 0)
            def _():
                fac_load(level).wait()

            acc[...] = jnp.zeros_like(acc)

            def half_pass(which):
                @pl.when(which == 0)
                def _():
                    def keep(u):
                        kl[h, 0, level * 8 + u] = unfold(
                            ko[slot, h, u].astype(F32).reshape(16, 16, Q)).astype(BF)
                    each(0, 8, keep)

                @pl.when(which == 1)
                def _():
                    pltpu.make_async_copy(kx.at[slot, h], kx.at[slot, h], f6_recv.at[level, h]).wait()

                    def keep(u):
                        kl[h, 1, level * 8 + u] = unfold(
                            kx[slot, h, u].astype(F32).reshape(16, 16, Q)).astype(BF)
                    each(0, 8, keep)

                half = lax.rem(core + which, 2)

                def add(k, carry):
                    dep = deps_ref[level, 0, k]
                    r = lax.rem(dep, 8)
                    at = dep - r + lax.rem(r, 2) * 4 + lax.div(r, 2)
                    value = kl[h, which, at]
                    value = jnp.where(k < counts_ref[0, 0, level], value, jnp.zeros_like(value))
                    block = fac[level, k, :, half_cols(half)]
                    acc[...] += lax.dot_general(
                        value, block, (((1,), (1,)), ((), ())), preferred_element_type=F32)
                    return carry

                lax.fori_loop(0, SPD, add, 0, unroll=True)

            each(0, 2, half_pass)
            part[h] = fold(acc[...]).astype(BF).reshape(4, 4, 16, H)
            start_each(0, 15, part_copy(level, h))
            f1r[level, h, y, x] = part[h, y, x]
            wait_bytes(124, line_send.at[h])
            wait_bytes(192, axis_send.at[h])
            wait_bytes(192, axis_send.at[h])
            pltpu.make_async_copy(ko.at[slot, h], ko.at[slot, h], sib_send.at[h]).wait()

        each(0, 2, finish)
        for half in (0, 1):
            which = lax.rem(core + half, 2)
            outs[0, level, :, half * H : (half + 1) * H] = rows_of_both(
                [kl[h, which, level * 8 + me].astype(F32) for h in (0, 1)])
        result_out(0, forward_ref, level).start()
        dinv_load(m).wait()

        def next_level(h):
            wait_bytes(120, f1_recv.at[level, h])
            wait_bytes(120, plane_send.at[h])
            total = unfold(jnp.sum(
                f1r[level, h].astype(F32).reshape(16, 16, H), axis=0, keepdims=True))
            solve_forward(m, h, (rhs_f[m, h] - total).astype(BF))

            @pl.when(level < LEV - 2)
            def _():
                gather_start(m, h)

            @pl.when(level == LEV - 2)
            def _():
                fw3[h, y, x] = fold(fshare[LEV - 1, h])[0].astype(BF)
                solve_backward(LEV - 1, h, fshare[LEV - 1, h].astype(BF))

        each(0, 2, next_level)

    rhs_load(0).wait()

    def split_rhs(level):
        both = rhs_v[level].astype(F32)
        rhs_f[level, 0] = both[:8]
        rhs_f[level, 1] = both[8:]

    split_rhs(0)
    dinv_load(0).wait()
    each(0, 2, lambda h: solve_forward(0, h, rhs_f[0, h].astype(BF)))
    pl.semaphore_wait(barrier, 64)
    each(0, 2, lambda h: gather_start(0, h))

    def late(level):
        rhs_load(level).wait()
        split_rhs(level)

    each(1, LEV, late)
    each(0, LEV - 1, prepare)
    each(0, LEV - 1, forward_level)

    def take_plane(level, h):
        wait_bytes(120, ag_recv.at[level, h])
        wait_bytes(120, plane_send.at[h])

    def plane_result(at, ref, level, parts):
        outs[at, level] = rows_of_both([unfold(v.astype(F32).reshape(16, 16, H)) for v in parts])
        result_out(at, ref, level).start()

    def backward_level(it):
        level = LEV - 1 - it
        low = level - 1

        def far_first(kk):
            return near_first(3 - kk)

        def gathered(h, unit, which):
            value = a[h, which, 0, last[0, low * 8 + unit]]
            for m in range(1, LEV - 1):
                value = value + a[h, which, m, last[m, low * 8 + unit]]
            return fold(value)

        def pair(h, unit):
            return send(sb.at[h, unit], sr.at[h, unit], sib_send.at[h],
                        sib_recv.at[low, h, unit], device(0, 0, 0, 1))

        def rs1(h, p, k, i):
            zc = rem4(z + k)
            if p == 0:
                src, to = os.at[h, zc, :, rem4(x + i)], device(i, 0, 0, 0)
            else:
                src, to = os.at[h, 4 + zc, rem4(y + i)], device(0, i, 0, 0)
            return send(src, r1.at[h, p, i - 1, zc], axis_send.at[h], rs1_recv.at[low, h, p, k], to)

        def rs2(h, o):
            k, n, i = lax.div(o, 8), lax.rem(lax.div(o, 4), 2), near_first(rem4(o))
            to = lax.rem(core + n, 2)
            at = rem4(x * to + y * (1 - to) + i)
            return send(
                s2.at[h, to, rem4(z + k), at], rr.at[low, h, core, k, i], line_send.at[h],
                rs2_recv.at[low, h], device(i * to, i * (1 - to), k, n))

        def terms(h):
            take_plane(level, h)
            sfull[h] = unfold(solg[level, h].astype(F32).reshape(16, 16, H)).astype(BF)

            def to_sibling(q):
                unit = lax.rem(q, 2) * 4 + rem4(z + far_first(lax.div(q, 2)))
                sb[h, unit] = gathered(h, unit, 0).astype(BF).reshape(4, 4, 16, Q)
                pair(h, unit).start()

            def contributions(which):
                half = lax.rem(core + 1 + which, 2)

                def slot(k, carry):
                    block = fac[low, k, :, half_cols(half)]
                    term = jnp.dot(sfull[h], block, preferred_element_type=F32)
                    a[h, which, low, k] = term + a[h, which, low, prev[low, k]]
                    return carry

                lax.fori_loop(0, SPD, slot, 0, unroll=True)

                @pl.when(which == 0)
                def _():
                    each(0, 8, to_sibling)

            each(0, 2, contributions)

            def merge(kk):
                k = far_first(kk)
                zc = rem4(z + k)
                for p in (0, 1):
                    unit = p * 4 + zc
                    pair(h, unit).wait_recv()
                    both = gathered(h, unit, 1) + sr[h, unit].astype(F32).reshape(16, 16, Q)
                    os[h, unit] = both.astype(BF).reshape(4, 4, 16, Q)
                    start_each(1, 4, lambda v: rs1(h, p, k, v))

            each(0, 4, merge)

        each(0, 2, terms)

        @pl.when(it == 0)
        def _():
            each(0, 2, lambda h: start_each(0, 15, fw3_copy(h)))

        plane_result(1, solution_ref, level, [solg[level, h] for h in (0, 1)])

        def fold_axis(h):
            def chunk(kk):
                k = far_first(kk)
                zc = rem4(z + k)
                for p in (0, 1):
                    wait_bytes(48, rs1_recv.at[low, h, p, k])
                    value = os[h, zc, :, x] if p == 0 else os[h, 4 + zc, y]
                    value = value.astype(F32)
                    for i in range(3):
                        value = value + r1[h, p, i, zc].astype(F32)
                    s2[h, p, zc] = value.astype(BF)
                first = jnp.where(kk == 3, 1, 0)
                start_each(first, 8, lambda q: rs2(h, k * 8 + q))

            each(0, 4, chunk)
            rr[low, h, core, 0, 0] = s2[h, core, z, line]

        each(0, 2, fold_axis)

        def solve(h):
            wait_bytes(124, rs2_recv.at[low, h])
            sums = [
                unfold(jnp.sum(
                    rr[low, h, half].astype(F32).reshape(16, 16, Q), axis=0, keepdims=True))
                for half in range(2)]
            total = jnp.concatenate(sums, axis=1)
            solve_backward(low, h, (fshare[low, h] - total).astype(BF))
            wait_bytes(124, line_send.at[h])
            wait_bytes(192, axis_send.at[h])
            wait_bytes(192, axis_send.at[h])
            pltpu.make_async_copy(sb.at[h], sb.at[h], sib_send.at[h]).wait()

        each(0, 2, solve)

    each(0, LEV - 1, backward_level)
    for h in (0, 1):
        wait_bytes(120, fw3_recv.at[h])
        wait_bytes(120, fw3_send.at[h])
    plane_result(0, forward_ref, LEV - 1, [fw3[h] for h in (0, 1)])
    each(0, 2, lambda h: take_plane(0, h))
    plane_result(1, solution_ref, 0, [solg[0, h] for h in (0, 1)])
    each(0, LEV, lambda level: result_out(0, forward_ref, level).wait())
    each(0, LEV, lambda level: result_out(1, solution_ref, level).wait())


def shards(rhs, dinv, factor, deps, counts, sizes):
    any_spec = pl.BlockSpec(memory_space=pl.ANY)
    smem = pl.BlockSpec(memory_space=pltpu.SMEM)
    dma = pltpu.SemaphoreType.DMA
    block = (2, 8, 4, 4, 16, Q)
    forward, solved = pl.pallas_call(
        kernel,
        out_shape=[jax.ShapeDtypeStruct((LEV, H, W), BF)] * 2,
        in_specs=[any_spec] * 3 + [smem] * 3,
        out_specs=[any_spec] * 2,
        scratch_shapes=[
            pltpu.VMEM((LEV, 16, W), BF),
            pltpu.VMEM((LEV, 2, 8, W), F32),
            pltpu.VMEM((LEV, W, W), BF),
            pltpu.VMEM((LEV - 1, SPD, W, W), BF),
            pltpu.VMEM((2,) + block, BF),
            pltpu.VMEM((2,) + block, BF),
            pltpu.VMEM((2, 2, 24, Q, H), BF),
            pltpu.VMEM((LEV, 2, 2, 16, Q), BF),
            pltpu.VMEM((LEV, 2, 8, W), F32),
            pltpu.VMEM((2, 4, 4, 16, H), BF),
            pltpu.VMEM((Q, W), F32),
            pltpu.VMEM((LEV - 1, 2, 4, 4, 16, H), BF),
            pltpu.VMEM((2, 2, LEV - 1, SPD + 1, Q, H), F32),
            pltpu.VMEM(block, BF),
            pltpu.VMEM(block, BF),
            pltpu.VMEM(block, BF),
            pltpu.VMEM((2, 2, 3, 4, 4, 16, Q), BF),
            pltpu.VMEM((2, 2, 4, 4, 16, Q), BF),
            pltpu.VMEM((LEV - 1, 2, 2, 4, 4, 16, Q), BF),
            pltpu.VMEM((LEV, 2, 4, 4, 16, H), BF),
            pltpu.VMEM((2, Q, W), BF),
            pltpu.VMEM((2, 4, 4, 16, H), BF),
            pltpu.VMEM((2, LEV, H, W), BF),
            pltpu.VMEM((W, 128), F32),
            pltpu.SMEM((LEV - 1, SPD), jnp.int32),
            pltpu.SMEM((LEV - 1, 24), jnp.int32),
            dma((LEV,)), dma((LEV,)), dma((LEV - 1,)), dma((2, LEV)),
            dma((2,)), dma((2,)), dma((LEV - 1, 2)), dma((LEV, 2)), dma((2,)),
            dma((2,)), dma((LEV - 1, 2, 4)), dma((LEV - 1, 2)),
            dma((2,)), dma((LEV - 1, 2, 4)), dma((LEV - 1, 2, 2, 4)),
            dma((2,)), dma((LEV - 1, 2)), dma((LEV - 1, 2, 8)),
        ],
        compiler_params=pltpu.CompilerParams(
            collective_id=0, has_side_effects=True, vmem_limit_bytes=61 << 20),
        name="levels",
    )(rhs, dinv, factor, deps, counts.transpose(1, 2, 0), sizes.T)
    return forward[:, None], solved[:, None]


def solution(mesh):
    placed = (
        P(None, "row", None, None),
        P(None, "row", None, None),
        P(None, "row", ("layer", "col"), None, None),
        P(None, "row", ("layer", "col")),
        P(None, "row", ("layer", "col")),
        P(None, "row"),
    )
    return jax.shard_map(
        shards,
        mesh=mesh,
        in_specs=placed,
        out_specs=(P(None, "row", None, None), P(None, "row", None, None)),
        check_vma=False,
    )
```

```python
import jax
import jax.numpy as jnp
from jax import lax
from jax.experimental import pallas as pl
from jax.experimental.pallas import tpu as pltpu
from jax.sharding import PartitionSpec as P

MESH = pl.DeviceIdType.MESH
BF = jnp.bfloat16
F32 = jnp.float32
LEV = 4
SPD = 12
W = 512
H = 256
Q = 128


def rem4(v):
    return lax.rem(v, 4)


def near_first(v):
    return v + lax.div(v, 2) * (5 - 2 * v)


def fold(v):
    n, c = v.shape
    t = v.reshape(n // 8, 8, c)
    return jnp.concatenate([t[:, :, : c // 2], t[:, :, c // 2 :]], axis=1)


def unfold(v):
    n, _, c = v.shape
    return jnp.concatenate([v[:, :8], v[:, 8:]], axis=2).reshape(n * 8, 2 * c)


def kernel(
    rhs_ref, dinv_ref, factor_ref, deps_ref, counts_ref, sizes_ref,
    forward_ref, solution_ref,
    rhs_v, rhs_f, dinv_v, fac, ko, kx, kl,
    share, fshare, part, acc, f1r,
    a, sb, sr, os, r1, s2, rr, solg, sfull, fw3, outs,
    spare, prev, last,
    rhs_sem, dinv_sem, fac_sem, out_sem,
    plane_send, fw3_send, f1_recv, ag_recv, fw3_recv,
    line_send, s1_recv, rs2_recv,
    axis_send, f5_recv, rs1_recv,
    sib_send, f6_recv, sib_recv,
):
    layer, row, col = lax.axis_index("layer"), lax.axis_index("row"), lax.axis_index("col")
    x = rem4(col)
    y = layer * 2 + lax.div(col, 4)
    z = lax.div(row, 2)
    core = lax.rem(row, 2)
    other = 1 - core
    me = core * 4 + z
    line = x * core + y * other

    def device(i, j, k, n):
        xx, yy, zz, cc = rem4(x + i), rem4(y + j), rem4(z + k), lax.rem(core + n, 2)
        return (lax.div(yy, 2), zz * 2 + cc, lax.rem(yy, 2) * 4 + xx)

    def send(src, dst, send_sem, recv_sem, to):
        return pltpu.make_async_remote_copy(
            src_ref=src, dst_ref=dst, send_sem=send_sem, recv_sem=recv_sem,
            device_id=to, device_id_type=MESH,
        )

    def each(low, high, body):
        def step(at, carry):
            body(at)
            return carry
        lax.fori_loop(low, high, step, 0)

    def start_each(low, high, copy):
        def step(at, carry):
            copy(at).start()
            return carry
        lax.fori_loop(low, high, step, 0, unroll=True)

    def wait_bytes(kib, sem):
        some = spare.at[pl.ds(0, kib * 2)]
        pltpu.make_async_copy(some, some, sem).wait()

    def half_cols(half):
        return pl.ds(pl.multiple_of(half * H, H), H)

    barrier = pltpu.get_barrier_semaphore()

    def greet(i, j, k, n):
        pl.semaphore_signal(barrier, inc=1, device_id=device(i, j, k, n), device_id_type=MESH)

    def rhs_load(level):
        mine = pl.ds(pl.multiple_of((y * 4 + x) * 16, 16), 16)
        return pltpu.make_async_copy(rhs_ref.at[level, 0, mine], rhs_v.at[level], rhs_sem.at[level])

    def dinv_load(level):
        return pltpu.make_async_copy(dinv_ref.at[level, 0], dinv_v.at[level], dinv_sem.at[level])

    def fac_load(m):
        return pltpu.make_async_copy(factor_ref.at[m, 0], fac.at[m], fac_sem.at[m])

    def start_loads(level):
        rhs_load(level).start()
        dinv_load(level).start()

    start_loads(0)
    for o in range(1, 16):
        greet(o % 4, o // 4, 0, 0)
    for o in range(4, 32):
        greet(0, o % 4, o // 8, o // 4 % 2)
    for o in range(3, 24):
        greet(1 + o % 3, 0, o // 6, o // 3 % 2)
    each(1, LEV, start_loads)
    each(0, LEV - 1, lambda m: fac_load(m).start())

    def live_rows(level):
        return (lax.broadcasted_iota(jnp.int32, (1, W), 1) < sizes_ref[0, level]).astype(F32)

    def plane_copy(o, src, dst, send_sem, recv_sem):
        i, j = near_first(rem4(15 - o)), near_first(3 - lax.div(o, 4))
        return send(src(rem4(y + j), rem4(x + i)), dst, send_sem, recv_sem, device(i, j, 0, 0))

    def part_copy(level, h):
        return lambda o: plane_copy(
            o, lambda gy, gx: part.at[h, gy, gx], f1r.at[level, h, y, x],
            plane_send.at[h], f1_recv.at[level, h])

    def sol_copy(level, h):
        return lambda o: plane_copy(
            o, lambda gy, gx: solg.at[level, h, y, x], solg.at[level, h, y, x],
            plane_send.at[h], ag_recv.at[level, h])

    def fw3_copy(h):
        return lambda o: plane_copy(
            o, lambda gy, gx: fw3.at[h, y, x], fw3.at[h, y, x], fw3_send.at[h], fw3_recv.at[h])

    def prepare(m):
        count = counts_ref[0, 0, m]
        keys = [jnp.where(k < count, deps_ref[m, 0, k], 255) for k in range(SPD)]
        for k in range(SPD):
            at = jnp.int32(SPD)
            for j in range(k):
                at = jnp.where(keys[j] == keys[k], j, at)
            prev[m, k] = at

        def target(t):
            unit = lax.rem(t, 8)
            name = lax.div(t, 8) * 8 + rem4(unit) * 2 + lax.div(unit, 4)
            at = jnp.int32(SPD)
            for k in range(SPD):
                at = jnp.where(keys[k] == name, k, at)
            last[m, t] = at

        each(0, 24, target)
        for h in (0, 1):
            for which in (0, 1):
                a[h, which, m, SPD] = jnp.zeros((Q, H), F32)

    def solve_forward(level, h, resid):
        product = lax.dot_general(
            resid, dinv_v[level], (((1,), (1,)), ((), ())), preferred_element_type=F32)
        solved = (product * live_rows(level)).astype(BF).astype(F32)
        fshare[level, h] = solved
        share[level, h, 0] = fold(solved[:, :H])[0].astype(BF)
        share[level, h, 1] = fold(solved[:, H:])[0].astype(BF)

    def solve_backward(level, h, resid):
        product = jnp.dot(resid, dinv_v[level], preferred_element_type=F32)
        solg[level, h, y, x] = fold(product * live_rows(level))[0].astype(BF)
        start_each(0, 15, sol_copy(level, h))

    def gather_start(level, h):
        def s1(o):
            k, n, i = near_first(lax.div(o, 8)), lax.rem(lax.div(o, 4), 2), near_first(rem4(o))
            half = lax.rem(core + n, 2)
            return send(
                share.at[level, h, half], ko.at[lax.rem(level, 2), h, me, y, x], line_send.at[h],
                s1_recv.at[level, h, k], device(i * core, i * other, k, n))

        pltpu.make_async_copy(
            share.at[level, h, core], ko.at[lax.rem(level, 2), h, me, y, x],
            s1_recv.at[level, h, 0]).start()
        start_each(1, 32, s1)

    def result_out(at, ref, level):
        return pltpu.make_async_copy(outs.at[at, level], ref.at[level], out_sem.at[at, level])

    def rows_of_both(parts):
        both = [v.reshape(16, 8, v.shape[-1]) for v in parts]
        return jnp.concatenate(both, axis=1).astype(BF).reshape(H, both[0].shape[-1])

    def forward_level(level):
        slot = lax.rem(level, 2)
        m = level + 1

        def evens(ref, h, zc, at):
            return ref.at[slot, h, zc, :, at]

        def odds(ref, h, zc, at):
            return ref.at[slot, h, 4 + zc, at]

        def f5(h, p, k, i):
            zc = rem4(z + 4 - k)
            if p == 0:
                src, to = evens(ko, h, zc, x), device(i, 0, 0, 0)
            else:
                src, to = odds(ko, h, zc, y), device(0, i, 0, 0)
            return send(src, src, axis_send.at[h], f5_recv.at[level, h, k], to)

        def f6(h, p, k, i):
            zc = rem4(z + 4 - k)
            if p == 0:
                at = rem4(x + 4 - i)
                src, dst = evens(ko, h, zc, at), evens(kx, h, zc, at)
            else:
                at = rem4(y + 4 - i)
                src, dst = odds(ko, h, zc, at), odds(kx, h, zc, at)
            return send(src, dst, sib_send.at[h], f6_recv.at[level, h], device(0, 0, 0, 1))

        def spread(h):
            def chunk(kk):
                k = near_first(kk)
                wait_bytes(32, s1_recv.at[level, h, k])

                for i in (2, 1, 3):
                    f5(h, 0, k, i).start()
                    f5(h, 1, k, i).start()
                f6(h, 0, k, 0).start()
                f6(h, 1, k, 0).start()

            each(0, 4, chunk)

        each(0, 2, spread)

        def finish(h):
            def relay(kk):
                k = near_first(kk)
                wait_bytes(96, f5_recv.at[level, h, k])

                for i in (1, 3, 2):
                    f6(h, 0, k, i).start()
                    f6(h, 1, k, i).start()

            each(0, 4, relay)

            @pl.when(h == 0)
            def _():
                fac_load(level).wait()

            acc[...] = jnp.zeros_like(acc)

            def half_pass(which):
                @pl.when(which == 0)
                def _():
                    def keep(u):
                        kl[h, 0, level * 8 + u] = unfold(
                            ko[slot, h, u].astype(F32).reshape(16, 16, Q)).astype(BF)
                    each(0, 8, keep)

                @pl.when(which == 1)
                def _():
                    pltpu.make_async_copy(kx.at[slot, h], kx.at[slot, h], f6_recv.at[level, h]).wait()

                    def keep(u):
                        kl[h, 1, level * 8 + u] = unfold(
                            kx[slot, h, u].astype(F32).reshape(16, 16, Q)).astype(BF)
                    each(0, 8, keep)

                half = lax.rem(core + which, 2)

                def add(k, carry):
                    dep = deps_ref[level, 0, k]
                    r = lax.rem(dep, 8)
                    at = dep - r + lax.rem(r, 2) * 4 + lax.div(r, 2)
                    value = kl[h, which, at]
                    value = jnp.where(k < counts_ref[0, 0, level], value, jnp.zeros_like(value))
                    block = fac[level, k, :, half_cols(half)]
                    acc[...] += lax.dot_general(
                        value, block, (((1,), (1,)), ((), ())), preferred_element_type=F32)
                    return carry

                lax.fori_loop(0, SPD, add, 0, unroll=True)

            each(0, 2, half_pass)
            part[h] = fold(acc[...]).astype(BF).reshape(4, 4, 16, H)
            start_each(0, 15, part_copy(level, h))
            f1r[level, h, y, x] = part[h, y, x]
            wait_bytes(124, line_send.at[h])
            wait_bytes(192, axis_send.at[h])
            wait_bytes(192, axis_send.at[h])
            pltpu.make_async_copy(ko.at[slot, h], ko.at[slot, h], sib_send.at[h]).wait()

        each(0, 2, finish)
        for half in (0, 1):
            which = lax.rem(core + half, 2)
            outs[0, level, :, half * H : (half + 1) * H] = rows_of_both(
                [kl[h, which, level * 8 + me].astype(F32) for h in (0, 1)])
        result_out(0, forward_ref, level).start()
        dinv_load(m).wait()

        def next_level(h):
            wait_bytes(120, f1_recv.at[level, h])
            wait_bytes(120, plane_send.at[h])
            total = unfold(jnp.sum(
                f1r[level, h].astype(F32).reshape(16, 16, H), axis=0, keepdims=True))
            solve_forward(m, h, (rhs_f[m, h] - total).astype(BF))

            @pl.when(level < LEV - 2)
            def _():
                gather_start(m, h)

            @pl.when(level == LEV - 2)
            def _():
                fw3[h, y, x] = fold(fshare[LEV - 1, h])[0].astype(BF)
                solve_backward(LEV - 1, h, fshare[LEV - 1, h].astype(BF))

        each(0, 2, next_level)

    rhs_load(0).wait()

    def split_rhs(level):
        both = rhs_v[level].astype(F32)
        rhs_f[level, 0] = both[:8]
        rhs_f[level, 1] = both[8:]

    split_rhs(0)
    dinv_load(0).wait()
    each(0, 2, lambda h: solve_forward(0, h, rhs_f[0, h].astype(BF)))
    pl.semaphore_wait(barrier, 64)
    each(0, 2, lambda h: gather_start(0, h))

    def late(level):
        rhs_load(level).wait()
        split_rhs(level)

    each(1, LEV, late)
    each(0, LEV - 1, prepare)
    each(0, LEV - 1, forward_level)

    def take_plane(level, h):
        wait_bytes(120, ag_recv.at[level, h])
        wait_bytes(120, plane_send.at[h])

    def plane_result(at, ref, level, parts):
        outs[at, level] = rows_of_both([unfold(v.astype(F32).reshape(16, 16, H)) for v in parts])
        result_out(at, ref, level).start()

    def backward_level(it):
        level = LEV - 1 - it
        low = level - 1

        def far_first(kk):
            return near_first(3 - kk)

        def gathered(h, unit, which):
            value = a[h, which, 0, last[0, low * 8 + unit]]
            for m in range(1, LEV - 1):
                value = value + a[h, which, m, last[m, low * 8 + unit]]
            return fold(value)

        def pair(h, unit):
            return send(sb.at[h, unit], sr.at[h, unit], sib_send.at[h],
                        sib_recv.at[low, h, unit], device(0, 0, 0, 1))

        def rs1(h, p, k, i):
            zc = rem4(z + k)
            if p == 0:
                src, to = os.at[h, zc, :, rem4(x + i)], device(i, 0, 0, 0)
            else:
                src, to = os.at[h, 4 + zc, rem4(y + i)], device(0, i, 0, 0)
            return send(src, r1.at[h, p, i - 1, zc], axis_send.at[h], rs1_recv.at[low, h, p, k], to)

        def rs2(h, o):
            k, n, i = lax.div(o, 8), lax.rem(lax.div(o, 4), 2), near_first(rem4(o))
            to = lax.rem(core + n, 2)
            at = rem4(x * to + y * (1 - to) + i)
            return send(
                s2.at[h, to, rem4(z + k), at], rr.at[low, h, core, k, i], line_send.at[h],
                rs2_recv.at[low, h], device(i * to, i * (1 - to), k, n))

        def terms(h):
            take_plane(level, h)
            sfull[h] = unfold(solg[level, h].astype(F32).reshape(16, 16, H)).astype(BF)

            def to_sibling(q):
                unit = lax.rem(q, 2) * 4 + rem4(z + far_first(lax.div(q, 2)))
                sb[h, unit] = gathered(h, unit, 0).astype(BF).reshape(4, 4, 16, Q)
                pair(h, unit).start()

            def contributions(which):
                half = lax.rem(core + 1 + which, 2)

                def slot(k, carry):
                    block = fac[low, k, :, half_cols(half)]
                    term = jnp.dot(sfull[h], block, preferred_element_type=F32)
                    a[h, which, low, k] = term + a[h, which, low, prev[low, k]]
                    return carry

                lax.fori_loop(0, SPD, slot, 0, unroll=True)

                @pl.when(which == 0)
                def _():
                    each(0, 8, to_sibling)

            each(0, 2, contributions)

            def merge(kk):
                k = far_first(kk)
                zc = rem4(z + k)
                for p in (0, 1):
                    unit = p * 4 + zc
                    pair(h, unit).wait_recv()
                    both = gathered(h, unit, 1) + sr[h, unit].astype(F32).reshape(16, 16, Q)
                    os[h, unit] = both.astype(BF).reshape(4, 4, 16, Q)
                    for i in (2, 1, 3):
                        rs1(h, p, k, i).start()

            each(0, 4, merge)

        each(0, 2, terms)

        def fold_axis(h):
            def chunk(kk):
                k = far_first(kk)
                zc = rem4(z + k)
                for p in (0, 1):
                    wait_bytes(48, rs1_recv.at[low, h, p, k])
                    value = os[h, zc, :, x] if p == 0 else os[h, 4 + zc, y]
                    value = value.astype(F32)
                    for i in range(3):
                        value = value + r1[h, p, i, zc].astype(F32)
                    s2[h, p, zc] = value.astype(BF)
                pl.when(kk < 3)(lambda: rs2(h, k * 8).start())
                start_each(1, 8, lambda q: rs2(h, k * 8 + q))

            each(0, 4, chunk)
            rr[low, h, core, 0, 0] = s2[h, core, z, line]

        each(0, 2, fold_axis)

        def solve(h):
            wait_bytes(124, rs2_recv.at[low, h])
            sums = [
                unfold(jnp.sum(
                    rr[low, h, half].astype(F32).reshape(16, 16, Q), axis=0, keepdims=True))
                for half in range(2)]
            total = jnp.concatenate(sums, axis=1)
            solve_backward(low, h, (fshare[low, h] - total).astype(BF))
            wait_bytes(124, line_send.at[h])
            wait_bytes(192, axis_send.at[h])
            wait_bytes(192, axis_send.at[h])
            pltpu.make_async_copy(sb.at[h], sb.at[h], sib_send.at[h]).wait()

        each(0, 2, solve)
        plane_result(1, solution_ref, level, [solg[level, h] for h in (0, 1)])

        @pl.when(it == 0)
        def _():
            each(0, 2, lambda h: start_each(0, 15, fw3_copy(h)))

    each(0, LEV - 1, backward_level)
    for h in (0, 1):
        wait_bytes(120, fw3_recv.at[h])
        wait_bytes(120, fw3_send.at[h])
    plane_result(0, forward_ref, LEV - 1, [fw3[h] for h in (0, 1)])
    each(0, 2, lambda h: take_plane(0, h))
    plane_result(1, solution_ref, 0, [solg[0, h] for h in (0, 1)])
    each(0, LEV, lambda level: result_out(0, forward_ref, level).wait())
    each(0, LEV, lambda level: result_out(1, solution_ref, level).wait())


def result_kernel(a_in, b_in, a_out, b_out, held, in_sem, out_sem):
    ways = [(at, src, dst, level) for level in range(LEV)
            for at, src, dst in ((0, a_in, a_out), (1, b_in, b_out))]
    for at, src, dst, level in ways:
        pltpu.make_async_copy(src.at[level], held.at[at, level], in_sem.at[at, level]).start()
    for at, src, dst, level in ways:
        pltpu.make_async_copy(src.at[level], held.at[at, level], in_sem.at[at, level]).wait()
        pltpu.make_async_copy(held.at[at, level], dst.at[level], out_sem.at[at, level]).start()
    for at, src, dst, level in ways:
        pltpu.make_async_copy(held.at[at, level], dst.at[level], out_sem.at[at, level]).wait()


def results(a, b):
    any_spec = pl.BlockSpec(memory_space=pl.ANY)
    sems = pltpu.SemaphoreType.DMA((2, LEV))
    return pl.pallas_call(
        result_kernel,
        out_shape=[jax.ShapeDtypeStruct(a.shape, a.dtype)] * 2,
        in_specs=[any_spec] * 2,
        out_specs=[any_spec] * 2,
        scratch_shapes=[pltpu.VMEM((2,) + a.shape, a.dtype), sems, sems],
        compiler_params=pltpu.CompilerParams(vmem_limit_bytes=60 << 20),
        name="results",
    )(a, b)


def shards(rhs, dinv, factor, deps, counts, sizes):
    any_spec = pl.BlockSpec(memory_space=pl.ANY)
    smem = pl.BlockSpec(memory_space=pltpu.SMEM)
    dma = pltpu.SemaphoreType.DMA
    block = (2, 8, 4, 4, 16, Q)
    forward, solved = pl.pallas_call(
        kernel,
        out_shape=[jax.ShapeDtypeStruct((LEV, H, W), BF)] * 2,
        in_specs=[any_spec] * 3 + [smem] * 3,
        out_specs=[any_spec] * 2,
        scratch_shapes=[
            pltpu.VMEM((LEV, 16, W), BF),
            pltpu.VMEM((LEV, 2, 8, W), F32),
            pltpu.VMEM((LEV, W, W), BF),
            pltpu.VMEM((LEV - 1, SPD, W, W), BF),
            pltpu.VMEM((2,) + block, BF),
            pltpu.VMEM((2,) + block, BF),
            pltpu.VMEM((2, 2, 24, Q, H), BF),
            pltpu.VMEM((LEV, 2, 2, 16, Q), BF),
            pltpu.VMEM((LEV, 2, 8, W), F32),
            pltpu.VMEM((2, 4, 4, 16, H), BF),
            pltpu.VMEM((Q, W), F32),
            pltpu.VMEM((LEV - 1, 2, 4, 4, 16, H), BF),
            pltpu.VMEM((2, 2, LEV - 1, SPD + 1, Q, H), F32),
            pltpu.VMEM(block, BF),
            pltpu.VMEM(block, BF),
            pltpu.VMEM(block, BF),
            pltpu.VMEM((2, 2, 3, 4, 4, 16, Q), BF),
            pltpu.VMEM((2, 2, 4, 4, 16, Q), BF),
            pltpu.VMEM((LEV - 1, 2, 2, 4, 4, 16, Q), BF),
            pltpu.VMEM((LEV, 2, 4, 4, 16, H), BF),
            pltpu.VMEM((2, Q, W), BF),
            pltpu.VMEM((2, 4, 4, 16, H), BF),
            pltpu.VMEM((2, LEV, H, W), BF),
            pltpu.VMEM((W, 128), F32),
            pltpu.SMEM((LEV - 1, SPD), jnp.int32),
            pltpu.SMEM((LEV - 1, 24), jnp.int32),
            dma((LEV,)), dma((LEV,)), dma((LEV - 1,)), dma((2, LEV)),
            dma((2,)), dma((2,)), dma((LEV - 1, 2)), dma((LEV, 2)), dma((2,)),
            dma((2,)), dma((LEV - 1, 2, 4)), dma((LEV - 1, 2)),
            dma((2,)), dma((LEV - 1, 2, 4)), dma((LEV - 1, 2, 2, 4)),
            dma((2,)), dma((LEV - 1, 2)), dma((LEV - 1, 2, 8)),
        ],
        compiler_params=pltpu.CompilerParams(
            collective_id=0, has_side_effects=True, vmem_limit_bytes=61 << 20),
        name="levels",
    )(rhs, dinv, factor, deps, counts.transpose(1, 2, 0), sizes.T)
    forward, solved = results(forward, solved)
    return forward[:, None], solved[:, None]


def solution(mesh):
    placed = (
        P(None, "row", None, None),
        P(None, "row", None, None),
        P(None, "row", ("layer", "col"), None, None),
        P(None, "row", ("layer", "col")),
        P(None, "row", ("layer", "col")),
        P(None, "row"),
    )
    return jax.shard_map(
        shards,
        mesh=mesh,
        in_specs=placed,
        out_specs=(P(None, "row", None, None), P(None, "row", None, None)),
        check_vma=False,
    )
```

```python
import jax
import jax.numpy as jnp
from jax import lax
from jax.experimental import pallas as pl
from jax.experimental.pallas import tpu as pltpu
from jax.sharding import PartitionSpec as P

MESH = pl.DeviceIdType.MESH
BF = jnp.bfloat16
F32 = jnp.float32
LEV = 4
SPD = 12
W = 512
H = 256
Q = 128


def rem4(v):
    return lax.rem(v, 4)


def near_first(v):
    return v + lax.div(v, 2) * (5 - 2 * v)


def fold(v):
    n, c = v.shape
    t = v.reshape(n // 8, 8, c)
    return jnp.concatenate([t[:, :, : c // 2], t[:, :, c // 2 :]], axis=1)


def unfold(v):
    n, _, c = v.shape
    return jnp.concatenate([v[:, :8], v[:, 8:]], axis=2).reshape(n * 8, 2 * c)


def kernel(
    rhs_ref, dinv_ref, factor_ref, deps_ref, counts_ref, sizes_ref,
    forward_ref, solution_ref,
    rhs_v, rhs_f, dinv_v, fac, ko, kx, kl,
    share, fshare, part, acc, f1r,
    a, sb, sr, os, r1, s2, rr, solg, sfull, fw3, outs,
    spare, prev, last,
    rhs_sem, dinv_sem, fac_sem, out_sem,
    plane_send, fw3_send, f1_recv, ag_recv, fw3_recv,
    line_send, s1_recv, rs2_recv,
    axis_send, f5_recv, rs1_recv,
    sib_send, f6_recv, sib_recv,
):
    layer, row, col = lax.axis_index("layer"), lax.axis_index("row"), lax.axis_index("col")
    x = rem4(col)
    y = layer * 2 + lax.div(col, 4)
    z = lax.div(row, 2)
    core = lax.rem(row, 2)
    other = 1 - core
    me = core * 4 + z
    line = x * core + y * other

    def device(i, j, k, n):
        xx, yy, zz, cc = rem4(x + i), rem4(y + j), rem4(z + k), lax.rem(core + n, 2)
        return (lax.div(yy, 2), zz * 2 + cc, lax.rem(yy, 2) * 4 + xx)

    def send(src, dst, send_sem, recv_sem, to):
        return pltpu.make_async_remote_copy(
            src_ref=src, dst_ref=dst, send_sem=send_sem, recv_sem=recv_sem,
            device_id=to, device_id_type=MESH,
        )

    def each(low, high, body):
        def step(at, carry):
            body(at)
            return carry
        lax.fori_loop(low, high, step, 0)

    def start_each(low, high, copy):
        def step(at, carry):
            copy(at).start()
            return carry
        lax.fori_loop(low, high, step, 0, unroll=True)

    def wait_bytes(kib, sem):
        some = spare.at[pl.ds(0, kib * 2)]
        pltpu.make_async_copy(some, some, sem).wait()

    def half_cols(half):
        return pl.ds(pl.multiple_of(half * H, H), H)

    barrier = pltpu.get_barrier_semaphore()

    def greet(i, j, k, n):
        pl.semaphore_signal(barrier, inc=1, device_id=device(i, j, k, n), device_id_type=MESH)

    def rhs_load(level):
        mine = pl.ds(pl.multiple_of((y * 4 + x) * 16, 16), 16)
        return pltpu.make_async_copy(rhs_ref.at[level, 0, mine], rhs_v.at[level], rhs_sem.at[level])

    def dinv_load(level):
        return pltpu.make_async_copy(dinv_ref.at[level, 0], dinv_v.at[level], dinv_sem.at[level])

    def fac_load(m):
        return pltpu.make_async_copy(factor_ref.at[m, 0], fac.at[m], fac_sem.at[m])

    def start_loads(level):
        rhs_load(level).start()
        dinv_load(level).start()

    start_loads(0)
    for o in range(1, 16):
        greet(o % 4, o // 4, 0, 0)
    for o in range(4, 32):
        greet(0, o % 4, o // 8, o // 4 % 2)
    for o in range(3, 24):
        greet(1 + o % 3, 0, o // 6, o // 3 % 2)
    each(1, LEV, start_loads)
    each(0, LEV - 1, lambda m: fac_load(m).start())

    def live_rows(level):
        return (lax.broadcasted_iota(jnp.int32, (1, W), 1) < sizes_ref[0, level]).astype(F32)

    def plane_copy(o, src, dst, send_sem, recv_sem):
        i, j = near_first(rem4(15 - o)), near_first(3 - lax.div(o, 4))
        return send(src(rem4(y + j), rem4(x + i)), dst, send_sem, recv_sem, device(i, j, 0, 0))

    def part_copy(level, h):
        return lambda o: plane_copy(
            o, lambda gy, gx: part.at[h, gy, gx], f1r.at[level, h, y, x],
            plane_send.at[h], f1_recv.at[level, h])

    def sol_copy(level, h):
        return lambda o: plane_copy(
            o, lambda gy, gx: solg.at[level, h, y, x], solg.at[level, h, y, x],
            plane_send.at[h], ag_recv.at[level, h])

    def fw3_copy(h):
        return lambda o: plane_copy(
            o, lambda gy, gx: fw3.at[h, y, x], fw3.at[h, y, x], fw3_send.at[h], fw3_recv.at[h])

    def prepare(m):
        count = counts_ref[0, 0, m]
        keys = [jnp.where(k < count, deps_ref[m, 0, k], 255) for k in range(SPD)]
        for k in range(SPD):
            at = jnp.int32(SPD)
            for j in range(k):
                at = jnp.where(keys[j] == keys[k], j, at)
            prev[m, k] = at

        def target(t):
            unit = lax.rem(t, 8)
            name = lax.div(t, 8) * 8 + rem4(unit) * 2 + lax.div(unit, 4)
            at = jnp.int32(SPD)
            for k in range(SPD):
                at = jnp.where(keys[k] == name, k, at)
            last[m, t] = at

        each(0, 24, target)
        for h in (0, 1):
            for which in (0, 1):
                a[h, which, m, SPD] = jnp.zeros((Q, H), F32)

    def solve_forward(level, h, resid):
        product = lax.dot_general(
            resid, dinv_v[level], (((1,), (1,)), ((), ())), preferred_element_type=F32)
        solved = (product * live_rows(level)).astype(BF).astype(F32)
        fshare[level, h] = solved
        share[level, h, 0] = fold(solved[:, :H])[0].astype(BF)
        share[level, h, 1] = fold(solved[:, H:])[0].astype(BF)

    def solve_backward(level, h, resid):
        product = jnp.dot(resid, dinv_v[level], preferred_element_type=F32)
        solg[level, h, y, x] = fold(product * live_rows(level))[0].astype(BF)
        start_each(0, 15, sol_copy(level, h))

    def gather_start(level, h):
        def s1(o):
            k, n, i = near_first(lax.div(o, 8)), lax.rem(lax.div(o, 4), 2), near_first(rem4(o))
            half = lax.rem(core + n, 2)
            return send(
                share.at[level, h, half], ko.at[lax.rem(level, 2), h, me, y, x], line_send.at[h],
                s1_recv.at[level, h, k], device(i * core, i * other, k, n))

        pltpu.make_async_copy(
            share.at[level, h, core], ko.at[lax.rem(level, 2), h, me, y, x],
            s1_recv.at[level, h, 0]).start()
        start_each(1, 32, s1)

    def result_out(at, ref, level):
        return pltpu.make_async_copy(outs.at[at, level], ref.at[level], out_sem.at[at, level])

    def rows_of_both(parts):
        both = [v.reshape(16, 8, v.shape[-1]) for v in parts]
        return jnp.concatenate(both, axis=1).astype(BF).reshape(H, both[0].shape[-1])

    def split_rhs(level):
        both = rhs_v[level].astype(F32)
        rhs_f[level, 0] = both[:8]
        rhs_f[level, 1] = both[8:]

    def late(level):
        rhs_load(level).wait()
        split_rhs(level)

    def forward_level(level):
        slot = lax.rem(level, 2)
        m = level + 1

        def evens(ref, h, zc, at):
            return ref.at[slot, h, zc, :, at]

        def odds(ref, h, zc, at):
            return ref.at[slot, h, 4 + zc, at]

        def f5(h, p, k, i):
            zc = rem4(z + 4 - k)
            if p == 0:
                src, to = evens(ko, h, zc, x), device(i, 0, 0, 0)
            else:
                src, to = odds(ko, h, zc, y), device(0, i, 0, 0)
            return send(src, src, axis_send.at[h], f5_recv.at[level, h, k], to)

        def f6(h, p, k, i):
            zc = rem4(z + 4 - k)
            if p == 0:
                at = rem4(x + 4 - i)
                src, dst = evens(ko, h, zc, at), evens(kx, h, zc, at)
            else:
                at = rem4(y + 4 - i)
                src, dst = odds(ko, h, zc, at), odds(kx, h, zc, at)
            return send(src, dst, sib_send.at[h], f6_recv.at[level, h], device(0, 0, 0, 1))

        def spread(h):
            def chunk(kk):
                k = near_first(kk)
                wait_bytes(32, s1_recv.at[level, h, k])

                for i in (2, 1, 3):
                    f5(h, 0, k, i).start()
                    f5(h, 1, k, i).start()
                f6(h, 0, k, 0).start()
                f6(h, 1, k, 0).start()

            each(0, 4, chunk)

        each(0, 2, spread)

        @pl.when(level == 0)
        def _():
            each(1, LEV, late)
            each(0, LEV - 1, prepare)

        def finish(h):
            def relay(kk):
                k = near_first(kk)
                wait_bytes(96, f5_recv.at[level, h, k])

                for i in (1, 3, 2):
                    f6(h, 0, k, i).start()
                    f6(h, 1, k, i).start()

            each(0, 4, relay)

            @pl.when(h == 0)
            def _():
                fac_load(level).wait()

            acc[...] = jnp.zeros_like(acc)

            def half_pass(which):
                @pl.when(which == 0)
                def _():
                    def keep(u):
                        kl[h, 0, level * 8 + u] = unfold(
                            ko[slot, h, u].astype(F32).reshape(16, 16, Q)).astype(BF)
                    each(0, 8, keep)

                @pl.when(which == 1)
                def _():
                    pltpu.make_async_copy(kx.at[slot, h], kx.at[slot, h], f6_recv.at[level, h]).wait()

                    def keep(u):
                        kl[h, 1, level * 8 + u] = unfold(
                            kx[slot, h, u].astype(F32).reshape(16, 16, Q)).astype(BF)
                    each(0, 8, keep)

                half = lax.rem(core + which, 2)

                def add(k, carry):
                    dep = deps_ref[level, 0, k]
                    r = lax.rem(dep, 8)
                    at = dep - r + lax.rem(r, 2) * 4 + lax.div(r, 2)
                    value = kl[h, which, at]
                    value = jnp.where(k < counts_ref[0, 0, level], value, jnp.zeros_like(value))
                    block = fac[level, k, :, half_cols(half)]
                    acc[...] += lax.dot_general(
                        value, block, (((1,), (1,)), ((), ())), preferred_element_type=F32)
                    return carry

                lax.fori_loop(0, SPD, add, 0, unroll=True)

            each(0, 2, half_pass)
            part[h] = fold(acc[...]).astype(BF).reshape(4, 4, 16, H)
            start_each(0, 15, part_copy(level, h))
            f1r[level, h, y, x] = part[h, y, x]
            wait_bytes(124, line_send.at[h])
            wait_bytes(192, axis_send.at[h])
            wait_bytes(192, axis_send.at[h])
            pltpu.make_async_copy(ko.at[slot, h], ko.at[slot, h], sib_send.at[h]).wait()

        each(0, 2, finish)
        for half in (0, 1):
            which = lax.rem(core + half, 2)
            outs[0, level, :, half * H : (half + 1) * H] = rows_of_both(
                [kl[h, which, level * 8 + me].astype(F32) for h in (0, 1)])
        result_out(0, forward_ref, level).start()
        dinv_load(m).wait()

        def next_level(h):
            wait_bytes(120, f1_recv.at[level, h])
            wait_bytes(120, plane_send.at[h])
            total = unfold(jnp.sum(
                f1r[level, h].astype(F32).reshape(16, 16, H), axis=0, keepdims=True))
            solve_forward(m, h, (rhs_f[m, h] - total).astype(BF))

            @pl.when(level < LEV - 2)
            def _():
                gather_start(m, h)

            @pl.when(level == LEV - 2)
            def _():
                fw3[h, y, x] = fold(fshare[LEV - 1, h])[0].astype(BF)
                solve_backward(LEV - 1, h, fshare[LEV - 1, h].astype(BF))

        each(0, 2, next_level)

    rhs_load(0).wait()

    split_rhs(0)
    dinv_load(0).wait()
    each(0, 2, lambda h: solve_forward(0, h, rhs_f[0, h].astype(BF)))
    pl.semaphore_wait(barrier, 64)
    each(0, 2, lambda h: gather_start(0, h))

    each(0, LEV - 1, forward_level)

    def take_plane(level, h):
        wait_bytes(120, ag_recv.at[level, h])
        wait_bytes(120, plane_send.at[h])

    def plane_result(at, ref, level, parts):
        outs[at, level] = rows_of_both([unfold(v.astype(F32).reshape(16, 16, H)) for v in parts])
        result_out(at, ref, level).start()

    def backward_level(it):
        level = LEV - 1 - it
        low = level - 1

        def far_first(kk):
            return near_first(3 - kk)

        def gathered(h, unit, which):
            value = a[h, which, 0, last[0, low * 8 + unit]]
            for m in range(1, LEV - 1):
                value = value + a[h, which, m, last[m, low * 8 + unit]]
            return fold(value)

        def pair(h, unit):
            return send(sb.at[h, unit], sr.at[h, unit], sib_send.at[h],
                        sib_recv.at[low, h, unit], device(0, 0, 0, 1))

        def rs1(h, p, k, i):
            zc = rem4(z + k)
            if p == 0:
                src, to = os.at[h, zc, :, rem4(x + i)], device(i, 0, 0, 0)
            else:
                src, to = os.at[h, 4 + zc, rem4(y + i)], device(0, i, 0, 0)
            return send(src, r1.at[h, p, i - 1, zc], axis_send.at[h], rs1_recv.at[low, h, p, k], to)

        def rs2(h, o):
            k, n, i = lax.div(o, 8), lax.rem(lax.div(o, 4), 2), near_first(rem4(o))
            to = lax.rem(core + n, 2)
            at = rem4(x * to + y * (1 - to) + i)
            return send(
                s2.at[h, to, rem4(z + k), at], rr.at[low, h, core, k, i], line_send.at[h],
                rs2_recv.at[low, h], device(i * to, i * (1 - to), k, n))

        def terms(h):
            take_plane(level, h)
            sfull[h] = unfold(solg[level, h].astype(F32).reshape(16, 16, H)).astype(BF)

            def to_sibling(q):
                unit = lax.rem(q, 2) * 4 + rem4(z + far_first(lax.div(q, 2)))
                sb[h, unit] = gathered(h, unit, 0).astype(BF).reshape(4, 4, 16, Q)
                pair(h, unit).start()

            def contributions(which):
                half = lax.rem(core + 1 + which, 2)

                def slot(k, carry):
                    block = fac[low, k, :, half_cols(half)]
                    term = jnp.dot(sfull[h], block, preferred_element_type=F32)
                    a[h, which, low, k] = term + a[h, which, low, prev[low, k]]
                    return carry

                lax.fori_loop(0, SPD, slot, 0, unroll=True)

                @pl.when(which == 0)
                def _():
                    each(0, 8, to_sibling)

            each(0, 2, contributions)

            def merge(kk):
                k = far_first(kk)
                zc = rem4(z + k)
                for p in (0, 1):
                    unit = p * 4 + zc
                    pair(h, unit).wait_recv()
                    both = gathered(h, unit, 1) + sr[h, unit].astype(F32).reshape(16, 16, Q)
                    os[h, unit] = both.astype(BF).reshape(4, 4, 16, Q)
                    for i in (2, 1, 3):
                        rs1(h, p, k, i).start()

            each(0, 4, merge)

        each(0, 2, terms)

        def fold_axis(h):
            def chunk(kk):
                k = far_first(kk)
                zc = rem4(z + k)
                for p in (0, 1):
                    wait_bytes(48, rs1_recv.at[low, h, p, k])
                    value = os[h, zc, :, x] if p == 0 else os[h, 4 + zc, y]
                    value = value.astype(F32)
                    for i in range(3):
                        value = value + r1[h, p, i, zc].astype(F32)
                    s2[h, p, zc] = value.astype(BF)
                pl.when(kk < 3)(lambda: rs2(h, k * 8).start())
                start_each(1, 8, lambda q: rs2(h, k * 8 + q))

            each(0, 4, chunk)
            rr[low, h, core, 0, 0] = s2[h, core, z, line]

        each(0, 2, fold_axis)

        def solve(h):
            wait_bytes(124, rs2_recv.at[low, h])
            sums = [
                unfold(jnp.sum(
                    rr[low, h, half].astype(F32).reshape(16, 16, Q), axis=0, keepdims=True))
                for half in range(2)]
            total = jnp.concatenate(sums, axis=1)
            solve_backward(low, h, (fshare[low, h] - total).astype(BF))
            wait_bytes(124, line_send.at[h])
            wait_bytes(192, axis_send.at[h])
            wait_bytes(192, axis_send.at[h])
            pltpu.make_async_copy(sb.at[h], sb.at[h], sib_send.at[h]).wait()

        each(0, 2, solve)
        plane_result(1, solution_ref, level, [solg[level, h] for h in (0, 1)])

        @pl.when(it == 0)
        def _():
            each(0, 2, lambda h: start_each(0, 15, fw3_copy(h)))

    each(0, LEV - 1, backward_level)
    for h in (0, 1):
        wait_bytes(120, fw3_recv.at[h])
        wait_bytes(120, fw3_send.at[h])
    plane_result(0, forward_ref, LEV - 1, [fw3[h] for h in (0, 1)])
    each(0, 2, lambda h: take_plane(0, h))
    plane_result(1, solution_ref, 0, [solg[0, h] for h in (0, 1)])
    each(0, LEV, lambda level: result_out(0, forward_ref, level).wait())
    each(0, LEV, lambda level: result_out(1, solution_ref, level).wait())


def result_kernel(a_in, b_in, a_out, b_out, held, in_sem, out_sem):
    ways = [(at, src, dst, level) for level in range(LEV)
            for at, src, dst in ((0, a_in, a_out), (1, b_in, b_out))]
    for at, src, dst, level in ways:
        pltpu.make_async_copy(src.at[level], held.at[at, level], in_sem.at[at, level]).start()
    for at, src, dst, level in ways:
        pltpu.make_async_copy(src.at[level], held.at[at, level], in_sem.at[at, level]).wait()
        pltpu.make_async_copy(held.at[at, level], dst.at[level], out_sem.at[at, level]).start()
    for at, src, dst, level in ways:
        pltpu.make_async_copy(held.at[at, level], dst.at[level], out_sem.at[at, level]).wait()


def results(a, b):
    any_spec = pl.BlockSpec(memory_space=pl.ANY)
    sems = pltpu.SemaphoreType.DMA((2, LEV))
    return pl.pallas_call(
        result_kernel,
        out_shape=[jax.ShapeDtypeStruct(a.shape, a.dtype)] * 2,
        in_specs=[any_spec] * 2,
        out_specs=[any_spec] * 2,
        scratch_shapes=[pltpu.VMEM((2,) + a.shape, a.dtype), sems, sems],
        compiler_params=pltpu.CompilerParams(vmem_limit_bytes=60 << 20),
        name="results",
    )(a, b)


def shards(rhs, dinv, factor, deps, counts, sizes):
    any_spec = pl.BlockSpec(memory_space=pl.ANY)
    smem = pl.BlockSpec(memory_space=pltpu.SMEM)
    dma = pltpu.SemaphoreType.DMA
    block = (2, 8, 4, 4, 16, Q)
    forward, solved = pl.pallas_call(
        kernel,
        out_shape=[jax.ShapeDtypeStruct((LEV, H, W), BF)] * 2,
        in_specs=[any_spec] * 3 + [smem] * 3,
        out_specs=[any_spec] * 2,
        scratch_shapes=[
            pltpu.VMEM((LEV, 16, W), BF),
            pltpu.VMEM((LEV, 2, 8, W), F32),
            pltpu.VMEM((LEV, W, W), BF),
            pltpu.VMEM((LEV - 1, SPD, W, W), BF),
            pltpu.VMEM((2,) + block, BF),
            pltpu.VMEM((2,) + block, BF),
            pltpu.VMEM((2, 2, 24, Q, H), BF),
            pltpu.VMEM((LEV, 2, 2, 16, Q), BF),
            pltpu.VMEM((LEV, 2, 8, W), F32),
            pltpu.VMEM((2, 4, 4, 16, H), BF),
            pltpu.VMEM((Q, W), F32),
            pltpu.VMEM((LEV - 1, 2, 4, 4, 16, H), BF),
            pltpu.VMEM((2, 2, LEV - 1, SPD + 1, Q, H), F32),
            pltpu.VMEM(block, BF),
            pltpu.VMEM(block, BF),
            pltpu.VMEM(block, BF),
            pltpu.VMEM((2, 2, 3, 4, 4, 16, Q), BF),
            pltpu.VMEM((2, 2, 4, 4, 16, Q), BF),
            pltpu.VMEM((LEV - 1, 2, 2, 4, 4, 16, Q), BF),
            pltpu.VMEM((LEV, 2, 4, 4, 16, H), BF),
            pltpu.VMEM((2, Q, W), BF),
            pltpu.VMEM((2, 4, 4, 16, H), BF),
            pltpu.VMEM((2, LEV, H, W), BF),
            pltpu.VMEM((W, 128), F32),
            pltpu.SMEM((LEV - 1, SPD), jnp.int32),
            pltpu.SMEM((LEV - 1, 24), jnp.int32),
            dma((LEV,)), dma((LEV,)), dma((LEV - 1,)), dma((2, LEV)),
            dma((2,)), dma((2,)), dma((LEV - 1, 2)), dma((LEV, 2)), dma((2,)),
            dma((2,)), dma((LEV - 1, 2, 4)), dma((LEV - 1, 2)),
            dma((2,)), dma((LEV - 1, 2, 4)), dma((LEV - 1, 2, 2, 4)),
            dma((2,)), dma((LEV - 1, 2)), dma((LEV - 1, 2, 8)),
        ],
        compiler_params=pltpu.CompilerParams(
            collective_id=0, has_side_effects=True, vmem_limit_bytes=61 << 20),
        name="levels",
    )(rhs, dinv, factor, deps, counts.transpose(1, 2, 0), sizes.T)
    forward, solved = results(forward, solved)
    return forward[:, None], solved[:, None]


def solution(mesh):
    placed = (
        P(None, "row", None, None),
        P(None, "row", None, None),
        P(None, "row", ("layer", "col"), None, None),
        P(None, "row", ("layer", "col")),
        P(None, "row", ("layer", "col")),
        P(None, "row"),
    )
    return jax.shard_map(
        shards,
        mesh=mesh,
        in_specs=placed,
        out_specs=(P(None, "row", None, None), P(None, "row", None, None)),
        check_vma=False,
    )
```
